32 devices in a mesh: row: 8 (over z, x), col: 4 (over y, core).
Axes of the slice: x: 2, y: 2, z: 4, core: 2. Of those that a mesh axis runs over, the one named last changes fastest.
Arguments:
- amplitudes: bfloat16 [8192, 768], P(('row', 'col')), may hold values from -6 to 6
- integrals: bfloat16 [8192, 768], P(('row', 'col')), may hold values from -0.21875 to 0.21875
- block_mask: int32 [64, 64], P('row'), may hold values from 0 to 1, as said below
- occ_energy: float32 [8], replicated, may hold values from -1.5 to -0.5
- vir_energy: float32 [1024], replicated, may hold values from 0.1 to 1.5
Outputs:
- update: bfloat16 [8, 4, 32, 128, 128], P('row', 'col')
The draws below stay inside these ranges and needn't reach their ends.
Inputs may be any that keep to these rules, and one draw needn't show every extreme that they name: block_mask is symmetric; among the 2 x 2 blocks (a, b) with the same a // 2 and b // 2 at most one is present, and for every a // 2 one block with b // 2 = a // 2 and b = a is present; for every cell (r, c) at most 32 of its blocks are present, with exactly 32 in some cell.
All inputs are finite; a program needn't handle non-finite values.
Results may differ from the reference program's by a relative error of at most 0.0049.
Values may be sent and summed in bfloat16 or wider, within the bound.
No kernel may reach another device: no remote copies, remote signals or barrier semaphores. Data moves between devices by JAX's collectives and lax.ppermute only.
A program may use at most 64 MiB of HBM per device.

```python
import jax
import jax.numpy as jnp
from jax import lax

BLOCK = 128
SHARD_BLOCKS = 2
KC = 768
NV = 1024
TILES = 192
ROW_GROUPS = 8
COL_GROUPS = 4
MB = 64
CAP = 32
N = 8192
NOCC = 8
N_COL = 4


def draw_block_mask(key, part):
    coarse = MB // SHARD_BLOCKS
    split = SHARD_BLOCKS
    limit = min(TILES, coarse)
    partners = limit - 1
    key_order = jax.random.fold_in(key, 11)
    key_level = jax.random.fold_in(key, 23)
    key_fine = jax.random.fold_in(key, 37)
    order = jax.random.permutation(key_order, coarse).astype(jnp.int32)
    places = jnp.arange(coarse, dtype=jnp.int32)
    level = jax.random.randint(key_level, (coarse,), 1, partners + 1).astype(jnp.int32)
    level = jnp.where(places <= partners, partners, level)
    offset = jnp.bitwise_xor(places[:, None], places[None, :])
    lowest = jnp.minimum(level[:, None], level[None, :])
    linked = (offset == 0) | (offset >= 1) & (offset <= lowest)
    inverse = jnp.argsort(order).astype(jnp.int32)
    graph = linked[inverse][:, inverse]
    first = places[:, None]
    second = places[None, :]
    source = first // N_COL * N_COL + second % N_COL
    target = second // N_COL * N_COL + first % N_COL
    coarse_mask = graph[source, target].astype(jnp.int32)
    choose = jax.random.randint(key_fine, (coarse, coarse), 0, split * split).astype(jnp.int32)
    upper = first <= second
    sym = jnp.where(upper, choose, choose.T)
    lead = sym // split
    trail = sym % split
    pick_row = jnp.where(first < second, lead, jnp.where(first > second, trail, lead))
    pick_col = jnp.where(first < second, trail, jnp.where(first > second, lead, lead))
    fine = jnp.arange(MB, dtype=jnp.int32)
    big_row = fine[:, None] // split
    big_col = fine[None, :] // split
    hit = (fine[:, None] % split == pick_row[big_row, big_col]) & (fine[None, :] % split == pick_col[big_row, big_col])
    return (coarse_mask[big_row, big_col] * hit.astype(jnp.int32)).astype(jnp.int32)


def shard_levels(rng, dims, cuts, least, largest):
    level, own = 1.0, jax.random.fold_in(rng, 6)
    for axis_at, parts in cuts:
        heights = jnp.exp(jax.random.uniform(jax.random.fold_in(own, axis_at), (parts,), jnp.float32, least / len(cuts), largest / len(cuts)))
        level = level * jnp.repeat(heights, dims[axis_at] // parts).reshape([-1 if axis == axis_at else 1 for axis in range(len(dims))])
    return level


def centred(rng, shape, deviation, bound, pieces=(), kind=jnp.bfloat16):
    drawn = deviation * jax.random.normal(rng, shape, jnp.float32)
    if pieces:
        drawn = drawn * shard_levels(rng, shape, pieces, -0.22, 0.18)
    return jnp.clip(drawn, -bound, bound).astype(kind)


def setup_inputs(seed: int = 0) -> dict:
    key_of = jax.random.split(jax.random.key(seed), 6)
    amplitudes = centred(key_of[0], (N, KC), 1.0, 6.0, ((0, 32),))
    integrals = centred(key_of[1], (N, KC), KC ** -0.5, 0.21875, ((0, 32),))
    block_mask = draw_block_mask(jax.random.fold_in(key_of[5], 71), 0)
    occ_energy = jnp.clip(jax.random.uniform(key_of[3], (NOCC,), jnp.float32, -1.5, -0.5), -1.5, -0.5)
    vir_energy = jnp.clip(jax.random.uniform(key_of[4], (NV,), jnp.float32, 0.1, 1.5), 0.1, 1.5)
    return {"amplitudes": amplitudes, "integrals": integrals, "block_mask": block_mask, "occ_energy": occ_energy, "vir_energy": vir_energy}


def slot_layout(block_mask, row_at, col_at, nrow, ncol, split, limit):
    rows_mask = lax.dynamic_slice_in_dim(block_mask, (row_at * ncol * split).astype(jnp.int32), ncol * split, 0)
    tile_mask = lax.dynamic_index_in_dim(rows_mask.reshape(ncol * split, nrow, ncol, split), col_at, 2, keepdims=False)
    flat = tile_mask.reshape(-1)
    wide = nrow * split
    cells = ncol * split * wide
    places = jnp.arange(cells, dtype=jnp.int32)
    keys = jnp.where(flat > 0, places, places + cells)
    picked = jnp.argsort(keys, stable=True)[:limit].astype(jnp.int32)
    present = flat[picked] > 0
    return picked // wide, picked % wide, present


def reference(amplitudes, integrals, block_mask, occ_energy, vir_energy):
    nrow = ROW_GROUPS
    ncol = COL_GROUPS
    split = SHARD_BLOCKS
    cells = nrow * ncol
    amp_blocks = amplitudes.reshape(MB, BLOCK, KC)
    int_blocks = integrals.reshape(MB, BLOCK, KC)
    gaps = (vir_energy[None, :] - occ_energy[:, None]).reshape(MB, BLOCK)

    def one_cell(cell):
        row_at = cell // ncol
        col_at = cell % ncol
        upick, vpick, present = slot_layout(block_mask, row_at, col_at, nrow, ncol, split, CAP)
        row_block = row_at * ncol * split + upick
        col_block = ((vpick // split) * ncol + col_at) * split + vpick % split
        direct = jnp.einsum("sik,sjk->sij", amp_blocks[row_block].astype(jnp.float32), int_blocks[col_block].astype(jnp.float32)).astype(jnp.bfloat16)
        mirror = jnp.einsum("sik,sjk->sij", amp_blocks[col_block].astype(jnp.float32), int_blocks[row_block].astype(jnp.float32)).astype(jnp.bfloat16)
        mirror = jnp.swapaxes(mirror, 1, 2)
        denom = gaps[row_block][:, :, None] + gaps[col_block][:, None, :]
        total = (direct.astype(jnp.float32) + mirror.astype(jnp.float32)) / denom
        return jnp.where(present[:, None, None], total, jnp.float32(0.0)).astype(jnp.bfloat16)

    result = lax.map(one_cell, jnp.arange(cells, dtype=jnp.int32))
    return result.reshape(nrow, ncol, CAP, BLOCK, BLOCK)
```

```python
import functools

import jax
import jax.numpy as jnp
import numpy as np
from jax import lax
from jax.experimental import pallas as pl
from jax.experimental.pallas import tpu as pltpu
from jax.sharding import PartitionSpec as P

BLOCK = 128
SHARD_BLOCKS = 2
TILES = 192


def ring_order(count):
    short = 1
    while short * short * 4 <= count:
        short *= 2
    if count % short or (count // short) % 2 or short == 1:
        return list(range(count))
    tall = count // short
    walk = [z * short for z in range(tall)]
    for at, z in enumerate(reversed(range(tall))):
        xs = range(1, short) if at % 2 == 0 else reversed(range(1, short))
        walk += [z * short + x for x in xs]
    return walk


def slot_table(rows_mask, row_at, col_at, order, ncol, split):
    nrow = len(order)
    place = {row: at for at, row in enumerate(order)}
    source = np.array([[order[(place[row] - s) % nrow] for s in range(nrow)] for row in range(nrow)], np.int32)
    tile = lax.dynamic_index_in_dim(
        rows_mask.reshape(ncol * split, nrow, ncol, split), col_at, 2, keepdims=False
    )
    flat = (tile.reshape(-1) > 0).astype(jnp.int32)
    before = (jnp.cumsum(flat) - flat).reshape(ncol, split, nrow, split)
    hit = flat.reshape(ncol, split, nrow, split)
    half = jnp.arange(split, dtype=jnp.int32)
    present = hit.sum((1, 3))
    lead = (hit * half[None, :, None, None]).sum((1, 3))
    trail = (hit * half[None, None, None, :]).sum((1, 3))
    slot = jnp.where(present > 0, (hit * before).sum((1, 3)), -1)
    at_u = jnp.arange(ncol, dtype=jnp.int32)[:, None]
    at_v = jnp.arange(nrow, dtype=jnp.int32)[None, :]
    block_a = (row_at * ncol + at_u) * split + lead
    block_b = (at_v * ncol + col_at) * split + trail
    table = jnp.stack([at_u * split + lead, trail, slot, block_a, block_b])
    mine = lax.dynamic_index_in_dim(jnp.asarray(source), row_at, 0, keepdims=False)
    return jnp.swapaxes(table[:, :, mine], 1, 2).reshape(-1)


def step_kernel(s, ncol, stride, tab, amp_a, int_a, amp_b, int_b, gaps, held, out, tile, sem):
    del held
    at = s * ncol + pl.program_id(0)
    slot = tab[2 * stride + at]

    @pl.when(slot >= 0)
    def _():
        nt = (((1,), (1,)), ((), ()))
        direct = lax.dot_general(amp_a[...], int_b[...], nt, preferred_element_type=jnp.float32)
        mirror = lax.dot_general(int_a[...], amp_b[...], nt, preferred_element_type=jnp.float32)
        gap_a = gaps[pl.ds(tab[3 * stride + at], 1), :]
        gap_b = gaps[pl.ds(tab[4 * stride + at], 1), :]
        block = tile.shape[0]
        denom = jnp.broadcast_to(gap_a, (block, block)).T + gap_b
        total = direct.astype(jnp.bfloat16).astype(jnp.float32) + mirror.astype(jnp.bfloat16).astype(jnp.float32)
        tile[...] = (total / denom).astype(jnp.bfloat16)
        copy = pltpu.make_async_copy(tile, out.at[slot], sem)
        copy.start()
        copy.wait()


def step(s, tab, amp_row, int_row, amp_b, int_b, gaps, out, ncol, nrow):
    width = amp_b.shape[1]
    stride = nrow * ncol

    def row_block(j, tab):
        return (tab[s * ncol + j], 0)

    def col_block(j, tab):
        return (tab[stride + s * ncol + j], 0)

    row_spec = pl.BlockSpec((BLOCK, width), row_block)
    col_spec = pl.BlockSpec((BLOCK, width), col_block)
    return pl.pallas_call(
        functools.partial(step_kernel, s, ncol, stride),
        grid_spec=pltpu.PrefetchScalarGridSpec(
            num_scalar_prefetch=1,
            grid=(ncol,),
            in_specs=[
                row_spec,
                row_spec,
                col_spec,
                col_spec,
                pl.BlockSpec(gaps.shape, lambda j, tab: (0, 0)),
                pl.BlockSpec(memory_space=pl.ANY),
            ],
            out_specs=pl.BlockSpec(memory_space=pl.ANY),
            scratch_shapes=[pltpu.VMEM((BLOCK, BLOCK), jnp.bfloat16), pltpu.SemaphoreType.DMA],
        ),
        out_shape=jax.ShapeDtypeStruct(out.shape, out.dtype),
        input_output_aliases={6: 0},
        cost_estimate=pl.CostEstimate(
            flops=4 * ncol * BLOCK * BLOCK * width, bytes_accessed=8 * ncol * BLOCK * width, transcendentals=0
        ),
        name="blocks",
    )(tab, amp_row, int_row, amp_b, int_b, gaps, out)


def shards(amplitudes, integrals, block_mask, occ_energy, vir_energy):
    nrow = lax.axis_size("row")
    ncol = lax.axis_size("col")
    split = SHARD_BLOCKS
    cells = nrow * ncol
    limit = min(TILES, cells)
    row_at = lax.axis_index("row")
    col_at = lax.axis_index("col")
    order = ring_order(nrow)
    ahead = [(order[p], order[(p + 1) % nrow]) for p in range(nrow)]
    behind = [(b, a) for a, b in ahead]
    far = nrow // 2
    amp = {0: amplitudes}
    ints = {0: integrals}
    with jax.named_scope("ring"):
        for s in range(1, far + 1):
            amp[s] = lax.ppermute(amp[s - 1], "row", ahead)
            if s < far or nrow % 2:
                amp[-s] = lax.ppermute(amp[1 - s], "row", behind)
                ints[s] = lax.ppermute(ints[s - 1], "row", ahead)
            ints[-s] = lax.ppermute(ints[1 - s], "row", behind)
        if nrow % 2 == 0 and nrow > 1:
            ints[far] = ints[-far]
    amp_row = lax.all_gather(amplitudes, "col", axis=0, tiled=True)
    int_row = lax.all_gather(integrals, "col", axis=0, tiled=True)
    tab = slot_table(block_mask, row_at, col_at, order, ncol, split)
    gaps = (vir_energy[None, :] - occ_energy[:, None]).reshape(cells * split, BLOCK)
    out = jnp.zeros((limit, BLOCK, BLOCK), jnp.bfloat16)
    out = step(0, tab, amp_row, int_row, amp[0], ints[0], gaps, out, ncol, nrow)
    for s in range(1, far + 1):
        out = step(s, tab, amp_row, int_row, amp[s], ints[s], gaps, out, ncol, nrow)
        if (nrow - s) % nrow != s:
            out = step(nrow - s, tab, amp_row, int_row, amp[-s], ints[-s], gaps, out, ncol, nrow)
    return out[None, None]


def solution(mesh):
    in_specs = (P(("row", "col"), None), P(("row", "col"), None), P("row", None), P(), P())
    out_specs = P("row", "col", None, None, None)
    return jax.shard_map(shards, mesh=mesh, in_specs=in_specs, out_specs=out_specs, check_vma=False)
```

```python
import functools

import jax
import jax.numpy as jnp
import numpy as np
from jax import lax
from jax.experimental import pallas as pl
from jax.experimental.pallas import tpu as pltpu
from jax.sharding import PartitionSpec as P

BLOCK = 128
SHARD_BLOCKS = 2
TILES = 192


def ring_order(count):
    short = 1
    while short * short * 4 <= count:
        short *= 2
    if count % short or (count // short) % 2 or short == 1:
        return list(range(count))
    tall = count // short
    walk = [z * short for z in range(tall)]
    for at, z in enumerate(reversed(range(tall))):
        xs = range(1, short) if at % 2 == 0 else reversed(range(1, short))
        walk += [z * short + x for x in xs]
    return walk


def table_kernel(ncol, nrow, split, where, mask, tab):
    cells = ncol * nrow
    col_at = where[1]

    def clear(at, carry):
        tab[at] = -1
        tab[cells + at] = 0
        tab[2 * cells + at] = 0
        return carry

    lax.fori_loop(0, cells, clear, 0)

    def rows(u, count):
        def cols(i, count):
            for trail in range(split):
                hit = mask[u, (i * ncol + col_at) * split + trail] > 0

                @pl.when(hit)
                def _():
                    at = lax.div(u, split) * nrow + i
                    tab[at] = count
                    tab[cells + at] = lax.rem(u, split)
                    tab[2 * cells + at] = trail

                count = count + hit.astype(jnp.int32)
            return count

        return lax.fori_loop(0, nrow, cols, count)

    lax.fori_loop(0, ncol * split, rows, jnp.int32(0))


def slot_table(where, mask, ncol, nrow, split):
    smem = pl.BlockSpec(memory_space=pltpu.SMEM)
    return pl.pallas_call(
        functools.partial(table_kernel, ncol, nrow, split),
        in_specs=[smem, smem],
        out_specs=smem,
        out_shape=jax.ShapeDtypeStruct((3 * ncol * nrow,), jnp.int32),
        name="slots",
    )(where, mask)


def step_kernel(s, ncol, nrow, split, where, source, tab, occ, vir, *refs):
    amp_row, int_row = refs[:ncol], refs[ncol : 2 * ncol]
    amp_b, int_b, _, out = refs[2 * ncol : 2 * ncol + 4]
    amp_a, int_a, amp_c, int_c, tiles, sem_a, sem_c, sem_o = refs[2 * ncol + 4 :]
    cells = ncol * nrow
    row_at, col_at = where[0], where[1]
    i = source[row_at * nrow + s]
    groups = vir.shape[0]

    def place(m):
        return jnp.bitwise_xor(col_at, m) * nrow + i

    loads = [pltpu.make_async_copy(amp_b, amp_c, sem_c.at[0]), pltpu.make_async_copy(int_b, int_c, sem_c.at[1])]
    row_loads = []
    for m in range(ncol):
        rows = pl.ds(pl.multiple_of(tab[cells + place(m)] * BLOCK, BLOCK), BLOCK)
        row_loads.append(
            (
                pltpu.make_async_copy(amp_row[m].at[rows], amp_a.at[m], sem_a.at[2 * m]),
                pltpu.make_async_copy(int_row[m].at[rows], int_a.at[m], sem_a.at[2 * m + 1]),
            )
        )
    for load in loads:
        load.start()
    for pair in row_loads:
        for load in pair:
            load.start()
    for load in loads:
        load.wait()
    nt = (((1,), (1,)), ((), ()))
    stores = []
    for m in range(ncol):
        at = place(m)
        slot = tab[at]
        lead = tab[cells + at]
        trail = tab[2 * cells + at]
        for load in row_loads[m]:
            load.wait()
        cols = pl.ds(pl.multiple_of(trail * BLOCK, BLOCK), BLOCK)
        direct = lax.dot_general(amp_a[m], int_c[cols, :], nt, preferred_element_type=jnp.float32)
        mirror = lax.dot_general(int_a[m], amp_c[cols, :], nt, preferred_element_type=jnp.float32)
        block_a = (row_at * ncol + jnp.bitwise_xor(col_at, m)) * split + lead
        block_b = (i * ncol + col_at) * split + trail
        gap_a = vir[pl.ds(lax.rem(block_a, groups), 1), :] - occ[lax.div(block_a, groups)]
        gap_b = vir[pl.ds(lax.rem(block_b, groups), 1), :] - occ[lax.div(block_b, groups)]
        denom = jnp.broadcast_to(gap_a, (BLOCK, BLOCK)).T + gap_b
        total = direct.astype(jnp.bfloat16).astype(jnp.float32) + mirror.astype(jnp.bfloat16).astype(jnp.float32)
        tiles[m] = (total / denom).astype(jnp.bfloat16)
        store = pltpu.make_async_copy(tiles.at[m], out.at[jnp.maximum(slot, 0)], sem_o.at[m])
        pl.when(slot >= 0)(store.start)
        stores.append((slot, store))
    for slot, store in stores:
        pl.when(slot >= 0)(store.wait)


def step(s, where, source, tab, occ, vir, amp_row, int_row, amp_b, int_b, out, ncol, nrow, split):
    rows, width = amp_b.shape
    smem = pl.BlockSpec(memory_space=pltpu.SMEM)
    hbm = pl.BlockSpec(memory_space=pl.ANY)
    return pl.pallas_call(
        functools.partial(step_kernel, s, ncol, nrow, split),
        in_specs=[smem, smem, smem, smem, pl.BlockSpec(memory_space=pltpu.VMEM)] + [hbm] * (2 * ncol + 3),
        out_specs=hbm,
        scratch_shapes=[
            pltpu.VMEM((ncol, BLOCK, width), jnp.bfloat16),
            pltpu.VMEM((ncol, BLOCK, width), jnp.bfloat16),
            pltpu.VMEM((rows, width), jnp.bfloat16),
            pltpu.VMEM((rows, width), jnp.bfloat16),
            pltpu.VMEM((ncol, BLOCK, BLOCK), jnp.bfloat16),
            pltpu.SemaphoreType.DMA((2 * ncol,)),
            pltpu.SemaphoreType.DMA((2,)),
            pltpu.SemaphoreType.DMA((ncol,)),
        ],
        out_shape=jax.ShapeDtypeStruct(out.shape, out.dtype),
        input_output_aliases={5 + 2 * ncol + 2: 0},
        compiler_params=pltpu.CompilerParams(vmem_limit_bytes=32 * 1024 * 1024),
        cost_estimate=pl.CostEstimate(
            flops=4 * ncol * BLOCK * BLOCK * width, bytes_accessed=16 * ncol * BLOCK * width, transcendentals=0
        ),
        name="blocks",
    )(where, source, tab, occ, vir, *amp_row, *int_row, amp_b, int_b, out)


def gather_cols(x, ncol):
    parts = [x]
    while len(parts) < ncol:
        bit = len(parts)
        pairs = [(c, c ^ bit) for c in range(ncol)]
        parts = parts + [lax.ppermute(part, "col", pairs) for part in parts]
    return parts


def shards(amplitudes, integrals, block_mask, occ_energy, vir_energy):
    nrow = lax.axis_size("row")
    ncol = lax.axis_size("col")
    split = SHARD_BLOCKS
    limit = min(TILES, nrow * ncol)
    where = jnp.stack([lax.axis_index("row"), lax.axis_index("col")]).astype(jnp.int32)
    order = ring_order(nrow)
    spot = {row: at for at, row in enumerate(order)}
    source = np.array([order[(spot[row] - s) % nrow] for row in range(nrow) for s in range(nrow)], np.int32)
    ahead = [(order[p], order[(p + 1) % nrow]) for p in range(nrow)]
    behind = [(b, a) for a, b in ahead]
    far = nrow // 2
    amp = {0: amplitudes}
    ints = {0: integrals}
    for s in range(1, far + 1):
        amp[s] = lax.ppermute(amp[s - 1], "row", ahead)
        if s < far or nrow % 2:
            amp[-s] = lax.ppermute(amp[1 - s], "row", behind)
            ints[s] = lax.ppermute(ints[s - 1], "row", ahead)
        ints[-s] = lax.ppermute(ints[1 - s], "row", behind)
    if nrow % 2 == 0:
        ints[far] = ints[-far]
    amp_row = gather_cols(amplitudes, ncol)
    int_row = gather_cols(integrals, ncol)
    tab = slot_table(where, block_mask, ncol, nrow, split)
    vir = vir_energy.reshape(-1, BLOCK)
    out = jnp.zeros((limit, BLOCK, BLOCK), jnp.bfloat16)
    steps = [(0, 0)]
    for s in range(1, far + 1):
        steps.append((s, s))
        if s != nrow - s:
            steps.append((nrow - s, -s))
    for s, key in steps:
        out = step(
            s, where, source, tab, occ_energy, vir, amp_row, int_row, amp[key], ints[key], out, ncol, nrow, split
        )
    return out[None, None]


def solution(mesh):
    in_specs = (P(("row", "col"), None), P(("row", "col"), None), P("row", None), P(), P())
    out_specs = P("row", "col", None, None, None)
    return jax.shard_map(shards, mesh=mesh, in_specs=in_specs, out_specs=out_specs, check_vma=False)
```

```python
import functools

import jax
import jax.numpy as jnp
import numpy as np
from jax import lax
from jax.experimental import pallas as pl
from jax.experimental.pallas import tpu as pltpu
from jax.sharding import PartitionSpec as P

BLOCK = 128
SHARD_BLOCKS = 2
TILES = 192


def ring_order(count):
    short = 1
    while short * short * 4 <= count:
        short *= 2
    if count % short or (count // short) % 2 or short == 1:
        return list(range(count))
    tall = count // short
    walk = [z * short for z in range(tall)]
    for at, z in enumerate(reversed(range(tall))):
        xs = range(1, short) if at % 2 == 0 else reversed(range(1, short))
        walk += [z * short + x for x in xs]
    return walk


def table_kernel(ncol, nrow, split, where, mask, tab):
    cells = ncol * nrow
    col_at = where[1]

    def clear(at, carry):
        tab[at] = -1
        tab[cells + at] = 0
        tab[2 * cells + at] = 0
        return carry

    lax.fori_loop(0, cells, clear, 0)

    def rows(u, count):
        def cols(i, count):
            for trail in range(split):
                hit = mask[u, (i * ncol + col_at) * split + trail] > 0

                @pl.when(hit)
                def _():
                    at = lax.div(u, split) * nrow + i
                    tab[at] = count
                    tab[cells + at] = lax.rem(u, split)
                    tab[2 * cells + at] = trail

                count = count + hit.astype(jnp.int32)
            return count

        return lax.fori_loop(0, nrow, cols, count)

    lax.fori_loop(0, ncol * split, rows, jnp.int32(0))


def slot_table(where, mask, ncol, nrow, split):
    smem = pl.BlockSpec(memory_space=pltpu.SMEM)
    return pl.pallas_call(
        functools.partial(table_kernel, ncol, nrow, split),
        in_specs=[smem, smem],
        out_specs=smem,
        out_shape=jax.ShapeDtypeStruct((3 * ncol * nrow,), jnp.int32),
        name="slots",
    )(where, mask)


def step_kernel(hops, ncol, nrow, split, where, source, tab, occ, vir, *refs):
    amp_row, int_row = refs[:ncol], refs[ncol : 2 * ncol]
    refs = refs[2 * ncol :]
    count = len(hops)
    amp_b, int_b = refs[:count], refs[count : 2 * count]
    _, out, amp_a, int_a, amp_c, int_c, tiles, sem_a, sem_c, sem_o = refs[2 * count :]
    cells = ncol * nrow
    row_at, col_at = where[0], where[1]
    groups = vir.shape[0]
    at, loads = {}, []
    for n, s in enumerate(hops):
        i = source[row_at * nrow + s]
        for m in range(ncol):
            at[n, m] = jnp.bitwise_xor(col_at, m) * nrow + i
            rows = pl.ds(pl.multiple_of(tab[cells + at[n, m]] * BLOCK, BLOCK), BLOCK)
            to = pl.ds(m * BLOCK, BLOCK)
            loads.append(pltpu.make_async_copy(amp_row[m].at[rows], amp_a.at[n, to], sem_a.at[n, 2 * m]))
            loads.append(pltpu.make_async_copy(int_row[m].at[rows], int_a.at[n, to], sem_a.at[n, 2 * m + 1]))
        loads.append(pltpu.make_async_copy(amp_b[n], amp_c.at[n], sem_c.at[n, 0]))
        loads.append(pltpu.make_async_copy(int_b[n], int_c.at[n], sem_c.at[n, 1]))
    for load in loads:
        load.start()
    for load in loads:
        load.wait()
    nt = (((1,), (1,)), ((), ()))
    stores = []
    for n, s in enumerate(hops):
        i = source[row_at * nrow + s]
        direct = lax.dot_general(amp_a[n], int_c[n], nt, preferred_element_type=jnp.float32)
        mirror = lax.dot_general(int_a[n], amp_c[n], nt, preferred_element_type=jnp.float32)
        total = direct.astype(jnp.bfloat16).astype(jnp.float32) + mirror.astype(jnp.bfloat16).astype(jnp.float32)
        for m in range(ncol):
            slot = tab[at[n, m]]
            lead = tab[cells + at[n, m]]
            trail = tab[2 * cells + at[n, m]]
            strip = total[m * BLOCK : (m + 1) * BLOCK]
            value = strip[:, :BLOCK]
            for part in range(1, split):
                value = jnp.where(trail == part, strip[:, part * BLOCK : (part + 1) * BLOCK], value)
            block_a = (row_at * ncol + jnp.bitwise_xor(col_at, m)) * split + lead
            block_b = (i * ncol + col_at) * split + trail
            gap_a = vir[pl.ds(lax.rem(block_a, groups), 1), :] - occ[lax.div(block_a, groups)]
            gap_b = vir[pl.ds(lax.rem(block_b, groups), 1), :] - occ[lax.div(block_b, groups)]
            denom = jnp.broadcast_to(gap_a, (BLOCK, BLOCK)).T + gap_b
            tiles[n, m] = (value / denom).astype(jnp.bfloat16)
            stores.append((slot, pltpu.make_async_copy(tiles.at[n, m], out.at[jnp.maximum(slot, 0)], sem_o.at[n, m])))
    for slot, store in stores:
        pl.when(slot >= 0)(store.start)
    for slot, store in stores:
        pl.when(slot >= 0)(store.wait)


def step(hops, where, source, tab, occ, vir, amp_row, int_row, amp_b, int_b, out, ncol, nrow, split):
    rows, width = amp_b[0].shape
    count = len(hops)
    smem = pl.BlockSpec(memory_space=pltpu.SMEM)
    hbm = pl.BlockSpec(memory_space=pl.ANY)
    held = 5 + 2 * ncol + 2 * count
    return pl.pallas_call(
        functools.partial(step_kernel, hops, ncol, nrow, split),
        in_specs=[smem, smem, smem, smem, pl.BlockSpec(memory_space=pltpu.VMEM)] + [hbm] * (2 * ncol + 2 * count + 1),
        out_specs=hbm,
        scratch_shapes=[
            pltpu.VMEM((count, ncol * BLOCK, width), jnp.bfloat16),
            pltpu.VMEM((count, ncol * BLOCK, width), jnp.bfloat16),
            pltpu.VMEM((count, rows, width), jnp.bfloat16),
            pltpu.VMEM((count, rows, width), jnp.bfloat16),
            pltpu.VMEM((count, ncol, BLOCK, BLOCK), jnp.bfloat16),
            pltpu.SemaphoreType.DMA((count, 2 * ncol)),
            pltpu.SemaphoreType.DMA((count, 2)),
            pltpu.SemaphoreType.DMA((count, ncol)),
        ],
        out_shape=jax.ShapeDtypeStruct(out.shape, out.dtype),
        input_output_aliases={held: 0},
        compiler_params=pltpu.CompilerParams(vmem_limit_bytes=40 * 1024 * 1024),
        cost_estimate=pl.CostEstimate(
            flops=8 * count * ncol * BLOCK * BLOCK * width,
            bytes_accessed=4 * count * (ncol * BLOCK + rows) * width,
            transcendentals=0,
        ),
        name="blocks",
    )(where, source, tab, occ, vir, *amp_row, *int_row, *amp_b, *int_b, out)


def gather_cols(x, ncol):
    parts = {0: x}
    bit = ncol // 2
    while bit:
        pairs = [(c, c ^ bit) for c in range(ncol)]
        parts.update({m ^ bit: lax.ppermute(part, "col", pairs) for m, part in list(parts.items())})
        bit //= 2
    return [parts[m] for m in range(ncol)]


def after(x, gate):
    return x if gate is None else lax.optimization_barrier((x, gate))[0]


def shards(amplitudes, integrals, block_mask, occ_energy, vir_energy):
    nrow = lax.axis_size("row")
    ncol = lax.axis_size("col")
    split = SHARD_BLOCKS
    limit = min(TILES, nrow * ncol)
    where = jnp.stack([lax.axis_index("row"), lax.axis_index("col")]).astype(jnp.int32)
    order = ring_order(nrow)
    spot = {row: at for at, row in enumerate(order)}
    source = np.array([order[(spot[row] - s) % nrow] for row in range(nrow) for s in range(nrow)], np.int32)
    ahead = [(order[p], order[(p + 1) % nrow]) for p in range(nrow)]
    behind = [(b, a) for a, b in ahead]
    tab = slot_table(where, block_mask, ncol, nrow, split)
    vir = vir_energy.reshape(-1, BLOCK)
    out = jnp.zeros((limit, BLOCK, BLOCK), jnp.bfloat16)

    def update(hops, amp_b, int_b, out):
        return step(
            hops, where, source, tab, occ_energy, vir, amp_row, int_row, amp_b, int_b, out, ncol, nrow, split
        )

    far = nrow // 2
    amp_up = amp_down = amplitudes
    int_up = int_down = integrals
    amp_row = int_row = None
    for s in range(1, far + 1):
        last = (amp_up, amp_down, int_up, int_down)
        gate = None if s == 1 else tab if s == 2 else out
        amp_up = lax.ppermute(after(amp_up, gate), "row", ahead)
        int_down = lax.ppermute(after(int_down, gate), "row", behind)
        if s < nrow - s:
            int_up = lax.ppermute(after(int_up, gate), "row", ahead)
            amp_down = lax.ppermute(after(amp_down, gate), "row", behind)
        if s == 1:
            amp_row = gather_cols(amplitudes, ncol)
            int_row = gather_cols(integrals, ncol)
        else:
            if s == 2:
                out = update((0,), (amplitudes,), (integrals,), out)
            out = update((s - 1, nrow - s + 1), (last[0], last[1]), (last[2], last[3]), out)
    if far == nrow - far:
        out = update((far,), (amp_up,), (int_down,), out)
    else:
        out = update((far, nrow - far), (amp_up, amp_down), (int_up, int_down), out)
    return out[None, None]


def solution(mesh):
    in_specs = (P(("row", "col"), None), P(("row", "col"), None), P("row", None), P(), P())
    out_specs = P("row", "col", None, None, None)
    return jax.shard_map(shards, mesh=mesh, in_specs=in_specs, out_specs=out_specs, check_vma=False)
```

```python
import functools

import jax
import jax.numpy as jnp
import numpy as np
from jax import lax
from jax.experimental import pallas as pl
from jax.experimental.pallas import tpu as pltpu
from jax.sharding import PartitionSpec as P

BLOCK = 128
SHARD_BLOCKS = 2
TILES = 192


def ring_order(count):
    short = 1
    while short * short * 4 <= count:
        short *= 2
    if count % short or (count // short) % 2 or short == 1:
        return list(range(count))
    tall = count // short
    walk = [z * short for z in range(tall)]
    for at, z in enumerate(reversed(range(tall))):
        xs = range(1, short) if at % 2 == 0 else reversed(range(1, short))
        walk += [z * short + x for x in xs]
    return walk


def table_kernel(ncol, nrow, split, where, mask, tab):
    cells = ncol * nrow
    col_at = where[1]

    def clear(at, carry):
        tab[at] = -1
        tab[cells + at] = 0
        tab[2 * cells + at] = 0
        return carry

    lax.fori_loop(0, cells, clear, 0)

    def rows(u, count):
        def cols(i, count):
            for trail in range(split):
                hit = mask[u, (i * ncol + col_at) * split + trail] > 0

                @pl.when(hit)
                def _():
                    at = lax.div(u, split) * nrow + i
                    tab[at] = count
                    tab[cells + at] = lax.rem(u, split)
                    tab[2 * cells + at] = trail

                count = count + hit.astype(jnp.int32)
            return count

        return lax.fori_loop(0, nrow, cols, count)

    lax.fori_loop(0, ncol * split, rows, jnp.int32(0))


def slot_table(where, mask, ncol, nrow, split):
    smem = pl.BlockSpec(memory_space=pltpu.SMEM)
    return pl.pallas_call(
        functools.partial(table_kernel, ncol, nrow, split),
        in_specs=[smem, smem],
        out_specs=smem,
        out_shape=jax.ShapeDtypeStruct((3 * ncol * nrow,), jnp.int32),
        name="slots",
    )(where, mask)


def step_kernel(hops, ncol, nrow, split, where, source, tab, occ, vir, *refs):
    amp_row, int_row = refs[:ncol], refs[ncol : 2 * ncol]
    refs = refs[2 * ncol :]
    count = len(hops)
    amp_b, int_b = refs[:count], refs[count : 2 * count]
    _, out, amp_a, int_a, amp_c, int_c, tiles, sem_a, sem_c, sem_o = refs[2 * count :]
    cells = ncol * nrow
    row_at, col_at = where[0], where[1]
    groups = vir.shape[0]
    at, loads = {}, []
    for n, s in enumerate(hops):
        i = source[row_at * nrow + s]
        first = [pltpu.make_async_copy(int_b[n], int_c.at[n], sem_c.at[n, 0])]
        second = [pltpu.make_async_copy(amp_b[n], amp_c.at[n], sem_c.at[n, 1])]
        for m in range(ncol):
            at[n, m] = jnp.bitwise_xor(col_at, m) * nrow + i
            rows = pl.ds(pl.multiple_of(tab[cells + at[n, m]] * BLOCK, BLOCK), BLOCK)
            to = pl.ds(m * BLOCK, BLOCK)
            first.append(pltpu.make_async_copy(amp_row[m].at[rows], amp_a.at[n, to], sem_a.at[n, 2 * m]))
            second.append(pltpu.make_async_copy(int_row[m].at[rows], int_a.at[n, to], sem_a.at[n, 2 * m + 1]))
        loads.append((first, second))
    for first, second in loads:
        for load in first + second:
            load.start()
    nt = (((1,), (1,)), ((), ()))
    stores = []
    for n, s in enumerate(hops):
        i = source[row_at * nrow + s]
        first, second = loads[n]
        denoms = []
        for m in range(ncol):
            block_a = (row_at * ncol + jnp.bitwise_xor(col_at, m)) * split + tab[cells + at[n, m]]
            block_b = (i * ncol + col_at) * split + tab[2 * cells + at[n, m]]
            gap_a = vir[pl.ds(lax.rem(block_a, groups), 1), :] - occ[lax.div(block_a, groups)]
            gap_b = vir[pl.ds(lax.rem(block_b, groups), 1), :] - occ[lax.div(block_b, groups)]
            denoms.append((gap_a, gap_b))
        for load in first:
            load.wait()
        direct = lax.dot_general(amp_a[n], int_c[n], nt, preferred_element_type=jnp.float32).astype(jnp.bfloat16)
        for load in second:
            load.wait()
        mirror = lax.dot_general(int_a[n], amp_c[n], nt, preferred_element_type=jnp.float32).astype(jnp.bfloat16)
        for m in range(ncol):
            slot = tab[at[n, m]]
            trail = tab[2 * cells + at[n, m]]
            mine = slice(m * BLOCK, (m + 1) * BLOCK)
            pair = [x[mine, :BLOCK].astype(jnp.float32) for x in (direct, mirror)]
            for part in range(1, split):
                cols = slice(part * BLOCK, (part + 1) * BLOCK)
                pair = [jnp.where(trail == part, x[mine, cols].astype(jnp.float32), y) for x, y in zip((direct, mirror), pair)]
            gap_a, gap_b = denoms[m]
            denom = jnp.broadcast_to(gap_a, (BLOCK, BLOCK)).T + gap_b
            tiles[n, m] = ((pair[0] + pair[1]) / denom).astype(jnp.bfloat16)
            store = pltpu.make_async_copy(tiles.at[n, m], out.at[jnp.maximum(slot, 0)], sem_o.at[n, m])
            pl.when(slot >= 0)(store.start)
            stores.append((slot, store))
    for slot, store in stores:
        pl.when(slot >= 0)(store.wait)


def step(hops, where, source, tab, occ, vir, amp_row, int_row, amp_b, int_b, out, ncol, nrow, split):
    rows, width = amp_b[0].shape
    count = len(hops)
    smem = pl.BlockSpec(memory_space=pltpu.SMEM)
    hbm = pl.BlockSpec(memory_space=pl.ANY)
    held = 5 + 2 * ncol + 2 * count
    return pl.pallas_call(
        functools.partial(step_kernel, hops, ncol, nrow, split),
        in_specs=[smem, smem, smem, smem, pl.BlockSpec(memory_space=pltpu.VMEM)] + [hbm] * (2 * ncol + 2 * count + 1),
        out_specs=hbm,
        scratch_shapes=[
            pltpu.VMEM((count, ncol * BLOCK, width), jnp.bfloat16),
            pltpu.VMEM((count, ncol * BLOCK, width), jnp.bfloat16),
            pltpu.VMEM((count, rows, width), jnp.bfloat16),
            pltpu.VMEM((count, rows, width), jnp.bfloat16),
            pltpu.VMEM((count, ncol, BLOCK, BLOCK), jnp.bfloat16),
            pltpu.SemaphoreType.DMA((count, 2 * ncol)),
            pltpu.SemaphoreType.DMA((count, 2)),
            pltpu.SemaphoreType.DMA((count, ncol)),
        ],
        out_shape=jax.ShapeDtypeStruct(out.shape, out.dtype),
        input_output_aliases={held: 0},
        compiler_params=pltpu.CompilerParams(vmem_limit_bytes=4 * (count + 1) * (ncol * BLOCK + rows) * (width + rows) + (4 << 20)),
        cost_estimate=pl.CostEstimate(
            flops=8 * count * ncol * BLOCK * BLOCK * width,
            bytes_accessed=4 * count * (ncol * BLOCK + rows) * width,
            transcendentals=0,
        ),
        name="blocks",
    )(where, source, tab, occ, vir, *amp_row, *int_row, *amp_b, *int_b, out)


def gather_cols(x, ncol):
    parts = {0: x}
    bit = ncol // 2
    while bit:
        pairs = [(c, c ^ bit) for c in range(ncol)]
        parts.update({m ^ bit: lax.ppermute(part, "col", pairs) for m, part in list(parts.items())})
        bit //= 2
    return [parts[m] for m in range(ncol)]


def after(x, gate):
    return x if gate is None else lax.optimization_barrier((x, gate))[0]


def shards(amplitudes, integrals, block_mask, occ_energy, vir_energy):
    nrow = lax.axis_size("row")
    ncol = lax.axis_size("col")
    split = SHARD_BLOCKS
    limit = min(TILES, nrow * ncol)
    where = jnp.stack([lax.axis_index("row"), lax.axis_index("col")]).astype(jnp.int32)
    order = ring_order(nrow)
    spot = {row: at for at, row in enumerate(order)}
    source = np.array([order[(spot[row] - s) % nrow] for row in range(nrow) for s in range(nrow)], np.int32)
    ahead = [(order[p], order[(p + 1) % nrow]) for p in range(nrow)]
    behind = [(b, a) for a, b in ahead]
    tab = slot_table(where, block_mask, ncol, nrow, split)
    vir = vir_energy.reshape(-1, BLOCK)
    out = jnp.zeros((limit, BLOCK, BLOCK), jnp.bfloat16)

    def update(hops, amp_b, int_b, out):
        return step(
            hops, where, source, tab, occ_energy, vir, amp_row, int_row, amp_b, int_b, out, ncol, nrow, split
        )

    far = nrow // 2
    amp_up = amp_down = amplitudes
    int_up = int_down = integrals
    amp_row = int_row = gate = lead_gate = None
    for s in range(1, far + 1):
        last = (amp_up, amp_down, int_up, int_down)
        amp_up = lax.ppermute(after(amp_up, lead_gate), "row", ahead)
        int_down = lax.ppermute(after(int_down, lead_gate), "row", behind)
        if s < nrow - s:
            int_up = lax.ppermute(after(int_up, gate), "row", ahead)
            amp_down = lax.ppermute(after(amp_down, gate), "row", behind)
        lead_gate = gate
        if s == 1:
            amp_row = gather_cols(amplitudes, ncol)
            int_row = gather_cols(integrals, ncol)
            gate = tab
        elif s == 2:
            out = update((0,), (amplitudes,), (integrals,), out)
            gate = out
            out = update((1, nrow - 1), last[:2], last[2:], out)
        else:
            gate = out
            out = update((s - 1, nrow - s + 1), last[:2], last[2:], out)
    if far == nrow - far:
        out = update((far,), (amp_up,), (int_down,), out)
    else:
        out = update((far, nrow - far), (amp_up, amp_down), (int_up, int_down), out)
    return out[None, None]


def solution(mesh):
    in_specs = (P(("row", "col"), None), P(("row", "col"), None), P("row", None), P(), P())
    out_specs = P("row", "col", None, None, None)
    return jax.shard_map(shards, mesh=mesh, in_specs=in_specs, out_specs=out_specs, check_vma=False)
```

```python
import functools

import jax
import jax.numpy as jnp
import numpy as np
from jax import lax
from jax.experimental import pallas as pl
from jax.experimental.pallas import tpu as pltpu
from jax.sharding import PartitionSpec as P

BLOCK = 128
SHARD_BLOCKS = 2
TILES = 192


def ring_order(count):
    short = 1
    while short * short * 4 <= count:
        short *= 2
    if count % short or (count // short) % 2 or short == 1:
        return list(range(count))
    tall = count // short
    walk = [z * short for z in range(tall)]
    for at, z in enumerate(reversed(range(tall))):
        xs = range(1, short) if at % 2 == 0 else reversed(range(1, short))
        walk += [z * short + x for x in xs]
    return walk


def table_kernel(ncol, nrow, split, where, mask, tab):
    cells = ncol * nrow
    col_at = where[1]

    def clear(at, carry):
        tab[at] = -1
        tab[cells + at] = 0
        tab[2 * cells + at] = 0
        return carry

    lax.fori_loop(0, cells, clear, 0)

    def rows(u, count):
        def cols(i, count):
            for trail in range(split):
                hit = mask[u, (i * ncol + col_at) * split + trail] > 0

                @pl.when(hit)
                def _():
                    at = lax.div(u, split) * nrow + i
                    tab[at] = count
                    tab[cells + at] = lax.rem(u, split)
                    tab[2 * cells + at] = trail

                count = count + hit.astype(jnp.int32)
            return count

        return lax.fori_loop(0, nrow, cols, count)

    lax.fori_loop(0, ncol * split, rows, jnp.int32(0))


def slot_table(where, mask, ncol, nrow, split):
    smem = pl.BlockSpec(memory_space=pltpu.SMEM)
    return pl.pallas_call(
        functools.partial(table_kernel, ncol, nrow, split),
        in_specs=[smem, smem],
        out_specs=smem,
        out_shape=jax.ShapeDtypeStruct((3 * ncol * nrow,), jnp.int32),
        name="slots",
    )(where, mask)


def step_kernel(hops, ncol, nrow, split, where, source, tab, occ, vir, *refs):
    amp_row, int_row = refs[:ncol], refs[ncol : 2 * ncol]
    refs = refs[2 * ncol :]
    count = len(hops)
    amp_b, int_b = refs[:count], refs[count : 2 * count]
    _, out, tiles, sem = refs[2 * count :]
    cells = ncol * nrow
    row_at, col_at = where[0], where[1]
    groups = vir.shape[0]
    nt = (((1,), (1,)), ((), ()))

    def half(index):
        return pl.ds(pl.multiple_of(index * BLOCK, BLOCK), BLOCK)

    def gap(block):
        return vir[pl.ds(lax.rem(block, groups), 1), :] - occ[lax.div(block, groups)]

    stores = []
    for n, s in enumerate(hops):
        i = source[row_at * nrow + s]
        for m in range(ncol):
            j = jnp.bitwise_xor(col_at, m)
            at = j * nrow + i
            lead, trail = tab[cells + at], tab[2 * cells + at]
            a, b = half(lead), half(trail)
            direct = lax.dot_general(amp_row[m][a, :], int_b[n][b, :], nt, preferred_element_type=jnp.float32)
            mirror = lax.dot_general(int_row[m][a, :], amp_b[n][b, :], nt, preferred_element_type=jnp.float32)
            gap_a = gap((row_at * ncol + j) * split + lead)
            gap_b = gap((i * ncol + col_at) * split + trail)
            denom = jnp.broadcast_to(gap_a, (BLOCK, BLOCK)).T + gap_b
            total = direct.astype(jnp.bfloat16).astype(jnp.float32) + mirror.astype(jnp.bfloat16).astype(jnp.float32)
            tiles[n, m] = (total / denom).astype(jnp.bfloat16)
            slot = tab[at]
            stores.append((slot, pltpu.make_async_copy(tiles.at[n, m], out.at[jnp.maximum(slot, 0)], sem.at[n, m])))
    for slot, store in stores:
        pl.when(slot >= 0)(store.start)
    for slot, store in stores:
        pl.when(slot >= 0)(store.wait)


def step(hops, where, source, tab, occ, vir, amp_row, int_row, amp_b, int_b, out, ncol, nrow, split):
    rows, width = amp_b[0].shape
    count = len(hops)
    smem = pl.BlockSpec(memory_space=pltpu.SMEM)
    vmem = pl.BlockSpec(memory_space=pltpu.VMEM)
    hbm = pl.BlockSpec(memory_space=pl.ANY)
    shard_count = 2 * ncol + 2 * count
    return pl.pallas_call(
        functools.partial(step_kernel, hops, ncol, nrow, split),
        in_specs=[smem, smem, smem, smem, vmem] + [vmem] * shard_count + [hbm],
        out_specs=hbm,
        scratch_shapes=[
            pltpu.VMEM((count, ncol, BLOCK, BLOCK), jnp.bfloat16),
            pltpu.SemaphoreType.DMA((count, ncol)),
        ],
        out_shape=jax.ShapeDtypeStruct(out.shape, out.dtype),
        input_output_aliases={5 + shard_count: 0},
        compiler_params=pltpu.CompilerParams(vmem_limit_bytes=2 * shard_count * rows * width + (4 << 20)),
        cost_estimate=pl.CostEstimate(
            flops=4 * count * ncol * BLOCK * BLOCK * width,
            bytes_accessed=4 * count * (ncol * BLOCK + rows) * width,
            transcendentals=0,
        ),
        name="blocks",
    )(where, source, tab, occ, vir, *amp_row, *int_row, *amp_b, *int_b, out)


def gather_cols(x, ncol):
    parts = {0: x}
    bit = ncol // 2
    while bit:
        pairs = [(c, c ^ bit) for c in range(ncol)]
        parts.update({m ^ bit: lax.ppermute(part, "col", pairs) for m, part in list(parts.items())})
        bit //= 2
    return [parts[m] for m in range(ncol)]


def after(x, gate):
    return x if gate is None else lax.optimization_barrier((x, gate))[0]


def shards(amplitudes, integrals, block_mask, occ_energy, vir_energy):
    nrow = lax.axis_size("row")
    ncol = lax.axis_size("col")
    split = SHARD_BLOCKS
    limit = min(TILES, nrow * ncol)
    where = jnp.stack([lax.axis_index("row"), lax.axis_index("col")]).astype(jnp.int32)
    order = ring_order(nrow)
    spot = {row: at for at, row in enumerate(order)}
    source = np.array([order[(spot[row] - s) % nrow] for row in range(nrow) for s in range(nrow)], np.int32)
    ahead = [(order[p], order[(p + 1) % nrow]) for p in range(nrow)]
    behind = [(b, a) for a, b in ahead]
    tab = slot_table(where, block_mask, ncol, nrow, split)
    vir = vir_energy.reshape(-1, BLOCK)
    out = jnp.zeros((limit, BLOCK, BLOCK), jnp.bfloat16)

    def update(hops, amp_b, int_b, out):
        return step(
            hops, where, source, tab, occ_energy, vir, amp_row, int_row, amp_b, int_b, out, ncol, nrow, split
        )

    far = nrow // 2
    amp_up = amp_down = amplitudes
    int_up = int_down = integrals
    outs = [out]
    for s in range(1, far + 1):
        last = (amp_up, amp_down, int_up, int_down)
        gate = outs[s - 2] if s >= 4 else None
        amp_up = lax.ppermute(after(amp_up, gate), "row", ahead)
        int_down = lax.ppermute(after(int_down, gate), "row", behind)
        if s < nrow - s:
            int_up = lax.ppermute(after(int_up, gate), "row", ahead)
            amp_down = lax.ppermute(after(amp_down, gate), "row", behind)
        if s == 1:
            amp_row = gather_cols(amplitudes, ncol)
            int_row = gather_cols(integrals, ncol)
            out = update((0,), (amplitudes,), (integrals,), out)
        else:
            out = update((s - 1, nrow - s + 1), last[:2], last[2:], out)
        outs.append(out)
    if far == nrow - far:
        out = update((far,), (amp_up,), (int_down,), out)
    else:
        out = update((far, nrow - far), (amp_up, amp_down), (int_up, int_down), out)
    return out[None, None]


def solution(mesh):
    in_specs = (P(("row", "col"), None), P(("row", "col"), None), P("row", None), P(), P())
    out_specs = P("row", "col", None, None, None)
    return jax.shard_map(shards, mesh=mesh, in_specs=in_specs, out_specs=out_specs, check_vma=False)
```

```python
import functools

import jax
import jax.numpy as jnp
import numpy as np
from jax import lax
from jax.experimental import pallas as pl
from jax.experimental.pallas import tpu as pltpu
from jax.sharding import PartitionSpec as P

BLOCK = 128
SHARD_BLOCKS = 2
TILES = 192


def ring_order(count):
    short = 1
    while short * short * 4 <= count:
        short *= 2
    if count % short or (count // short) % 2 or short == 1:
        return list(range(count))
    tall = count // short
    walk = [z * short for z in range(tall)]
    for at, z in enumerate(reversed(range(tall))):
        xs = range(1, short) if at % 2 == 0 else reversed(range(1, short))
        walk += [z * short + x for x in xs]
    return walk


def table_kernel(ncol, nrow, split, where, mask, tab):
    cells = ncol * nrow
    col_at = where[1]

    def clear(at, carry):
        tab[at] = -1
        tab[cells + at] = 0
        tab[2 * cells + at] = 0
        return carry

    lax.fori_loop(0, cells, clear, 0)

    def rows(u, count):
        def cols(i, count):
            for trail in range(split):
                hit = mask[u, (i * ncol + col_at) * split + trail] > 0

                @pl.when(hit)
                def _():
                    at = lax.div(u, split) * nrow + i
                    tab[at] = count
                    tab[cells + at] = lax.rem(u, split)
                    tab[2 * cells + at] = trail

                count = count + hit.astype(jnp.int32)
            return count

        return lax.fori_loop(0, nrow, cols, count)

    lax.fori_loop(0, ncol * split, rows, jnp.int32(0))


def slot_table(where, mask, ncol, nrow, split):
    smem = pl.BlockSpec(memory_space=pltpu.SMEM)
    return pl.pallas_call(
        functools.partial(table_kernel, ncol, nrow, split),
        in_specs=[smem, smem],
        out_specs=smem,
        out_shape=jax.ShapeDtypeStruct((3 * ncol * nrow,), jnp.int32),
        name="slots",
    )(where, mask)


def step_kernel(hops, spots, ncol, nrow, split, where, source, tab, occ, vir, *refs):
    kept = 1 + max(n for n, _ in spots.values())
    row_shards = refs[:kept]
    refs = refs[kept:]
    count = len(hops)
    rows = split * BLOCK
    amp_b, int_b = refs[:count], refs[count : 2 * count]
    _, out, tiles, sem = refs[2 * count :]
    cells = ncol * nrow
    row_at, col_at = where[0], where[1]
    groups = vir.shape[0]
    nt = (((1,), (1,)), ((), ()))

    def half(index):
        return pl.ds(pl.multiple_of(index * BLOCK, BLOCK), BLOCK)

    def gap(block):
        return vir[pl.ds(lax.rem(block, groups), 1), :] - occ[lax.div(block, groups)]

    stores = []
    for n, s in enumerate(hops):
        i = source[row_at * nrow + s]
        for m in range(ncol):
            j = jnp.bitwise_xor(col_at, m)
            at = j * nrow + i
            lead, trail = tab[cells + at], tab[2 * cells + at]
            a, b = half(lead), half(trail)
            held, q = row_shards[spots[m][0]], spots[m][1]
            amp_a, int_a = (held.at[pl.ds((2 * q + kind) * rows, rows)] for kind in (0, 1))
            direct = lax.dot_general(amp_a[a, :], int_b[n][b, :], nt, preferred_element_type=jnp.float32)
            mirror = lax.dot_general(int_a[a, :], amp_b[n][b, :], nt, preferred_element_type=jnp.float32)
            gap_a = gap((row_at * ncol + j) * split + lead)
            gap_b = gap((i * ncol + col_at) * split + trail)
            denom = jnp.broadcast_to(gap_a, (BLOCK, BLOCK)).T + gap_b
            total = direct.astype(jnp.bfloat16).astype(jnp.float32) + mirror.astype(jnp.bfloat16).astype(jnp.float32)
            tiles[n, m] = (total / denom).astype(jnp.bfloat16)
            slot = tab[at]
            stores.append((slot, pltpu.make_async_copy(tiles.at[n, m], out.at[jnp.maximum(slot, 0)], sem.at[n, m])))
    for slot, store in stores:
        pl.when(slot >= 0)(store.start)
    for slot, store in stores:
        pl.when(slot >= 0)(store.wait)


def step(hops, spots, where, source, tab, occ, vir, row_shards, amp_b, int_b, out, ncol, nrow, split):
    rows, width = amp_b[0].shape
    count = len(hops)
    smem = pl.BlockSpec(memory_space=pltpu.SMEM)
    vmem = pl.BlockSpec(memory_space=pltpu.VMEM)
    hbm = pl.BlockSpec(memory_space=pl.ANY)
    shard_count = len(row_shards) + 2 * count
    return pl.pallas_call(
        functools.partial(step_kernel, hops, spots, ncol, nrow, split),
        in_specs=[smem, smem, smem, smem, vmem] + [vmem] * shard_count + [hbm],
        out_specs=hbm,
        scratch_shapes=[
            pltpu.VMEM((count, ncol, BLOCK, BLOCK), jnp.bfloat16),
            pltpu.SemaphoreType.DMA((count, ncol)),
        ],
        out_shape=jax.ShapeDtypeStruct(out.shape, out.dtype),
        input_output_aliases={5 + shard_count: 0},
        compiler_params=pltpu.CompilerParams(vmem_limit_bytes=4 * (ncol + count) * rows * width + (4 << 20)),
        cost_estimate=pl.CostEstimate(
            flops=4 * count * ncol * BLOCK * BLOCK * width,
            bytes_accessed=4 * count * (ncol * BLOCK + rows) * width,
            transcendentals=0,
        ),
        name="blocks",
    )(where, source, tab, occ, vir, *row_shards, *amp_b, *int_b, out)


def gather_cols(x, ncol, held):
    arrays, spots = [x], {0: (0, 0)}
    bit = ncol // 2
    gate = None
    while bit:
        pairs = [(c, c ^ bit) for c in range(ncol)]
        every = arrays[0] if len(arrays) == 1 else jnp.concatenate(arrays)
        starts = np.cumsum([0] + [array.shape[0] // x.shape[0] for array in arrays])
        spots.update({m ^ bit: (len(arrays), int(starts[n]) + q) for m, (n, q) in list(spots.items())})
        arrays.append(lax.ppermute(after(every, gate), "col", pairs))
        gate = held
        bit //= 2
    return arrays, spots


def after(x, gate):
    return x if gate is None else lax.optimization_barrier((x, gate))[0]


def shards(amplitudes, integrals, block_mask, occ_energy, vir_energy):
    nrow = lax.axis_size("row")
    ncol = lax.axis_size("col")
    split = SHARD_BLOCKS
    limit = min(TILES, nrow * ncol)
    where = jnp.stack([lax.axis_index("row"), lax.axis_index("col")]).astype(jnp.int32)
    order = ring_order(nrow)
    spot = {row: at for at, row in enumerate(order)}
    source = np.array([order[(spot[row] - s) % nrow] for row in range(nrow) for s in range(nrow)], np.int32)
    ahead = [(order[p], order[(p + 1) % nrow]) for p in range(nrow)]
    behind = [(b, a) for a, b in ahead]
    tab = slot_table(where, block_mask, ncol, nrow, split)
    vir = vir_energy.reshape(-1, BLOCK)
    out = jnp.zeros((limit, BLOCK, BLOCK), jnp.bfloat16)

    def update(hops, amp_b, int_b, out):
        return step(hops, spots, where, source, tab, occ_energy, vir, row_shards, amp_b, int_b, out, ncol, nrow, split)

    far = nrow // 2
    amp_up = amp_down = amplitudes
    int_up = int_down = integrals
    outs = {}
    for s in range(1, far + 1):
        last = (amp_up, amp_down, int_up, int_down)
        gate = outs[s - 3] if s >= 4 else None
        amp_up = lax.ppermute(after(amp_up, gate), "row", ahead)
        int_down = lax.ppermute(after(int_down, gate), "row", behind)
        if s < nrow - s:
            int_up = lax.ppermute(after(int_up, gate), "row", ahead)
            amp_down = lax.ppermute(after(amp_down, gate), "row", behind)
        if s == min(2, far):
            both = jnp.concatenate([amplitudes, integrals])
            row_shards, spots = gather_cols(both, ncol, (amp_up, int_down, *last[1:3]))
            out = update((0,), (amplitudes,), (integrals,), out)
        if s >= 2:
            out = update((s - 1, nrow - s + 1), last[:2], last[2:], out)
            outs[s - 1] = out
    if far == nrow - far:
        out = update((far,), (amp_up,), (int_down,), out)
    else:
        out = update((far, nrow - far), (amp_up, amp_down), (int_up, int_down), out)
    return out[None, None]


def solution(mesh):
    in_specs = (P(("row", "col"), None), P(("row", "col"), None), P("row", None), P(), P())
    out_specs = P("row", "col", None, None, None)
    return jax.shard_map(shards, mesh=mesh, in_specs=in_specs, out_specs=out_specs, check_vma=False)
```

```python
import functools

import jax
import jax.numpy as jnp
import numpy as np
from jax import lax
from jax.experimental import pallas as pl
from jax.experimental.pallas import tpu as pltpu
from jax.sharding import PartitionSpec as P

BLOCK = 128
SHARD_BLOCKS = 2
TILES = 192


def ring_order(count):
    short = 1
    while short * short * 4 <= count:
        short *= 2
    if count % short or (count // short) % 2 or short == 1:
        return list(range(count))
    tall = count // short
    walk = [z * short for z in range(tall)]
    for at, z in enumerate(reversed(range(tall))):
        xs = range(1, short) if at % 2 == 0 else reversed(range(1, short))
        walk += [z * short + x for x in xs]
    return walk


def table_kernel(ncol, nrow, split, where, source, mask, tab):
    cells = ncol * nrow
    row_at, col_at = where[0], where[1]
    for s in range(nrow):
        tab[3 * cells + s] = source[row_at * nrow + s]
    tab[3 * cells + nrow] = row_at
    tab[3 * cells + nrow + 1] = col_at

    def clear(at, carry):
        tab[at] = -1
        tab[cells + at] = 0
        tab[2 * cells + at] = 0
        return carry

    lax.fori_loop(0, cells, clear, 0)

    def rows(u, count):
        def cols(i, count):
            for trail in range(split):
                hit = mask[u, (i * ncol + col_at) * split + trail] > 0

                @pl.when(hit)
                def _():
                    at = lax.div(u, split) * nrow + i
                    tab[at] = count
                    tab[cells + at] = lax.rem(u, split)
                    tab[2 * cells + at] = trail

                count = count + hit.astype(jnp.int32)
            return count

        return lax.fori_loop(0, nrow, cols, count)

    lax.fori_loop(0, ncol * split, rows, jnp.int32(0))


def slot_table(where, source, mask, ncol, nrow, split):
    smem = pl.BlockSpec(memory_space=pltpu.SMEM)
    return pl.pallas_call(
        functools.partial(table_kernel, ncol, nrow, split),
        in_specs=[smem, smem, smem],
        out_specs=smem,
        out_shape=jax.ShapeDtypeStruct((3 * ncol * nrow + nrow + 2,), jnp.int32),
        name="slots",
    )(where, source, mask)


def step_kernel(hops, spots, ncol, nrow, split, tab, occ, vir, *refs):
    kept = 1 + max(n for at in spots.values() for n, _ in at)
    row_shards = refs[:kept]
    refs = refs[kept:]
    count = len(hops)
    rows = split * BLOCK
    amp_b, int_b = refs[:count], refs[count : 2 * count]
    _, out, tiles, sem = refs[2 * count :]
    cells = ncol * nrow
    row_at, col_at = tab[3 * cells + nrow], tab[3 * cells + nrow + 1]
    groups = vir.shape[0]
    nt = (((1,), (1,)), ((), ()))

    def half(index):
        return pl.ds(pl.multiple_of(index * BLOCK, BLOCK), BLOCK)

    def gap(block):
        return vir[pl.ds(lax.rem(block, groups), 1), :] - occ[lax.div(block, groups)]

    stores = []
    for n, s in enumerate(hops):
        i = tab[3 * cells + s]
        for m in range(ncol):
            j = jnp.bitwise_xor(col_at, m)
            at = j * nrow + i
            lead, trail = tab[cells + at], tab[2 * cells + at]
            a, b = half(lead), half(trail)
            amp_a, int_a = (row_shards[n_at].at[pl.ds(q * rows, rows)] for n_at, q in spots[m])
            direct = lax.dot_general(amp_a[a, :], int_b[n][b, :], nt, preferred_element_type=jnp.float32)
            mirror = lax.dot_general(int_a[a, :], amp_b[n][b, :], nt, preferred_element_type=jnp.float32)
            gap_a = gap((row_at * ncol + j) * split + lead)
            gap_b = gap((i * ncol + col_at) * split + trail)
            denom = jnp.broadcast_to(gap_a, (BLOCK, BLOCK)).T + gap_b
            total = direct.astype(jnp.bfloat16).astype(jnp.float32) + mirror.astype(jnp.bfloat16).astype(jnp.float32)
            tiles[n, m] = (total / denom).astype(jnp.bfloat16)
            slot = tab[at]
            stores.append((slot, pltpu.make_async_copy(tiles.at[n, m], out.at[jnp.maximum(slot, 0)], sem.at[n, m])))
    for slot, store in stores:
        pl.when(slot >= 0)(store.start)
    for slot, store in stores:
        pl.when(slot >= 0)(store.wait)


def step(hops, spots, tab, occ, vir, row_shards, amp_b, int_b, out, ncol, nrow, split):
    rows, width = amp_b[0].shape
    count = len(hops)
    smem = pl.BlockSpec(memory_space=pltpu.SMEM)
    vmem = pl.BlockSpec(memory_space=pltpu.VMEM)
    hbm = pl.BlockSpec(memory_space=pl.ANY)
    shard_count = len(row_shards) + 2 * count
    return pl.pallas_call(
        functools.partial(step_kernel, hops, spots, ncol, nrow, split),
        in_specs=[smem, smem, vmem] + [vmem] * shard_count + [hbm],
        out_specs=hbm,
        scratch_shapes=[
            pltpu.VMEM((count, ncol, BLOCK, BLOCK), jnp.bfloat16),
            pltpu.SemaphoreType.DMA((count, ncol)),
        ],
        out_shape=jax.ShapeDtypeStruct(out.shape, out.dtype),
        input_output_aliases={3 + shard_count: 0},
        compiler_params=pltpu.CompilerParams(vmem_limit_bytes=4 * (ncol + count) * rows * width + (4 << 20)),
        cost_estimate=pl.CostEstimate(
            flops=4 * count * ncol * BLOCK * BLOCK * width,
            bytes_accessed=4 * count * (ncol * BLOCK + rows) * width,
            transcendentals=0,
        ),
        name="blocks",
    )(tab, occ, vir, *row_shards, *amp_b, *int_b, out)


def gather_cols(amplitudes, integrals, ncol, held):
    arrays, spots = [amplitudes, integrals], {0: ((0, 0), (1, 0))}
    rows = amplitudes.shape[0]
    bit = ncol // 2
    while bit:
        pairs = [(c, c ^ bit) for c in range(ncol)]
        if len(arrays) == 2:
            spots[bit] = ((2, 0), (3, 0))
            arrays.append(lax.ppermute(amplitudes, "col", pairs))
            arrays.append(lax.ppermute(after(integrals, arrays[2]), "col", pairs))
        else:
            starts = np.cumsum([0] + [array.shape[0] // rows for array in arrays])
            moved = {m ^ bit: tuple((len(arrays), int(starts[n]) + q) for n, q in at) for m, at in spots.items()}
            spots.update(moved)
            arrays.append(lax.ppermute(after(jnp.concatenate(arrays), held), "col", pairs))
        bit //= 2
    return arrays, spots


def after(x, gate):
    return x if gate is None else lax.optimization_barrier((x, gate))[0]


def shards(amplitudes, integrals, block_mask, occ_energy, vir_energy):
    nrow = lax.axis_size("row")
    ncol = lax.axis_size("col")
    split = SHARD_BLOCKS
    limit = min(TILES, nrow * ncol)
    where = jnp.stack([lax.axis_index("row"), lax.axis_index("col")]).astype(jnp.int32)
    order = ring_order(nrow)
    spot = {row: at for at, row in enumerate(order)}
    source = np.array([order[(spot[row] - s) % nrow] for row in range(nrow) for s in range(nrow)], np.int32)
    ahead = [(order[p], order[(p + 1) % nrow]) for p in range(nrow)]
    behind = [(b, a) for a, b in ahead]
    tab = slot_table(where, source, block_mask, ncol, nrow, split)
    vir = vir_energy.reshape(-1, BLOCK)
    out = jnp.zeros((limit, BLOCK, BLOCK), jnp.bfloat16)

    def update(hops, amp_b, int_b, out):
        return step(hops, spots, tab, occ_energy, vir, row_shards, amp_b, int_b, out, ncol, nrow, split)

    far = nrow // 2
    amp_up = amp_down = amplitudes
    int_up = int_down = integrals
    outs = {}
    for s in range(1, far + 1):
        last = (amp_up, amp_down, int_up, int_down)
        gate = outs[s - 3] if s >= 4 else None
        amp_up = lax.ppermute(after(amp_up, gate), "row", ahead)
        int_down = lax.ppermute(after(int_down, gate), "row", behind)
        if s < nrow - s:
            int_up = lax.ppermute(after(int_up, gate), "row", ahead)
            amp_down = lax.ppermute(after(amp_down, gate), "row", behind)
        if s == min(2, far):
            row_shards, spots = gather_cols(amplitudes, integrals, ncol, (amp_up, int_down, int_up, amp_down))
            out = update((0,), (amplitudes,), (integrals,), out)
        if s >= 2:
            out = update((s - 1, nrow - s + 1), last[:2], last[2:], out)
            outs[s - 1] = out
    if far == nrow - far:
        out = update((far,), (amp_up,), (int_down,), out)
    else:
        out = update((far, nrow - far), (amp_up, amp_down), (int_up, int_down), out)
    return out[None, None]


def solution(mesh):
    in_specs = (P(("row", "col"), None), P(("row", "col"), None), P("row", None), P(), P())
    out_specs = P("row", "col", None, None, None)
    return jax.shard_map(shards, mesh=mesh, in_specs=in_specs, out_specs=out_specs, check_vma=False)
```

```python
import functools

import jax
import jax.numpy as jnp
import numpy as np
from jax import lax
from jax.experimental import pallas as pl
from jax.experimental.pallas import tpu as pltpu
from jax.sharding import PartitionSpec as P

BLOCK = 128
SHARD_BLOCKS = 2
TILES = 192


def ring_order(count):
    short = 1
    while short * short * 4 <= count:
        short *= 2
    if count % short or (count // short) % 2 or short == 1:
        return list(range(count))
    tall = count // short
    walk = [z * short for z in range(tall)]
    for at, z in enumerate(reversed(range(tall))):
        xs = range(1, short) if at % 2 == 0 else reversed(range(1, short))
        walk += [z * short + x for x in xs]
    return walk


def table_kernel(ncol, nrow, split, where, source, mask, tab):
    cells = ncol * nrow
    row_at, col_at = where[0], where[1]
    for s in range(nrow):
        tab[3 * cells + s] = source[row_at * nrow + s]
    tab[3 * cells + nrow] = row_at
    tab[3 * cells + nrow + 1] = col_at

    def clear(at, carry):
        tab[at] = -1
        tab[cells + at] = 0
        tab[2 * cells + at] = 0
        return carry

    lax.fori_loop(0, cells, clear, 0)

    def rows(u, count):
        def cols(i, count):
            for trail in range(split):
                hit = mask[u, (i * ncol + col_at) * split + trail] > 0

                @pl.when(hit)
                def _():
                    at = lax.div(u, split) * nrow + i
                    tab[at] = count
                    tab[cells + at] = lax.rem(u, split)
                    tab[2 * cells + at] = trail

                count = count + hit.astype(jnp.int32)
            return count

        return lax.fori_loop(0, nrow, cols, count)

    lax.fori_loop(0, ncol * split, rows, jnp.int32(0))


def slot_table(where, source, mask, ncol, nrow, split):
    smem = pl.BlockSpec(memory_space=pltpu.SMEM)
    return pl.pallas_call(
        functools.partial(table_kernel, ncol, nrow, split),
        in_specs=[smem, smem, smem],
        out_specs=smem,
        out_shape=jax.ShapeDtypeStruct((3 * ncol * nrow + nrow + 2,), jnp.int32),
        name="slots",
    )(where, source, mask)


def step_kernel(hops, spots, ncol, nrow, split, tab, occ, vir, *refs):
    kept = 1 + max(n for at in spots.values() for n, _ in at)
    row_shards = refs[:kept]
    refs = refs[kept:]
    count = len(hops)
    rows = split * BLOCK
    amp_b, int_b = refs[:count], refs[count : 2 * count]
    _, out, tiles, sem = refs[2 * count :]
    cells = ncol * nrow
    row_at, col_at = tab[3 * cells + nrow], tab[3 * cells + nrow + 1]
    groups = vir.shape[0]
    nt = (((1,), (1,)), ((), ()))

    def half(index):
        return pl.ds(pl.multiple_of(index * BLOCK, BLOCK), BLOCK)

    def gap(block):
        return vir[pl.ds(lax.rem(block, groups), 1), :] - occ[lax.div(block, groups)]

    stores = []
    for n, s in enumerate(hops):
        i = tab[3 * cells + s]
        for m in range(ncol):
            j = jnp.bitwise_xor(col_at, m)
            at = j * nrow + i
            lead, trail = tab[cells + at], tab[2 * cells + at]
            a, b = half(lead), half(trail)
            amp_a, int_a = (row_shards[n_at].at[pl.ds(q * rows, rows)] for n_at, q in spots[m])
            direct = lax.dot_general(amp_a[a, :], int_b[n][b, :], nt, preferred_element_type=jnp.float32)
            mirror = lax.dot_general(int_a[a, :], amp_b[n][b, :], nt, preferred_element_type=jnp.float32)
            gap_a = gap((row_at * ncol + j) * split + lead)
            gap_b = gap((i * ncol + col_at) * split + trail)
            denom = jnp.broadcast_to(gap_a, (BLOCK, BLOCK)).T + gap_b
            total = direct.astype(jnp.bfloat16).astype(jnp.float32) + mirror.astype(jnp.bfloat16).astype(jnp.float32)
            tiles[n, m] = (total / denom).astype(jnp.bfloat16)
            slot = tab[at]
            stores.append((slot, pltpu.make_async_copy(tiles.at[n, m], out.at[jnp.maximum(slot, 0)], sem.at[n, m])))
    for slot, store in stores:
        pl.when(slot >= 0)(store.start)
    for slot, store in stores:
        pl.when(slot >= 0)(store.wait)


def step(hops, spots, tab, occ, vir, row_shards, amp_b, int_b, out, ncol, nrow, split):
    rows, width = amp_b[0].shape
    count = len(hops)
    smem = pl.BlockSpec(memory_space=pltpu.SMEM)
    vmem = pl.BlockSpec(memory_space=pltpu.VMEM)
    hbm = pl.BlockSpec(memory_space=pl.ANY)
    shard_count = len(row_shards) + 2 * count
    return pl.pallas_call(
        functools.partial(step_kernel, hops, spots, ncol, nrow, split),
        in_specs=[smem, smem, vmem] + [vmem] * shard_count + [hbm],
        out_specs=hbm,
        scratch_shapes=[
            pltpu.VMEM((count, ncol, BLOCK, BLOCK), jnp.bfloat16),
            pltpu.SemaphoreType.DMA((count, ncol)),
        ],
        out_shape=jax.ShapeDtypeStruct(out.shape, out.dtype),
        input_output_aliases={3 + shard_count: 0},
        compiler_params=pltpu.CompilerParams(vmem_limit_bytes=4 * (ncol + count) * rows * width + (4 << 20)),
        cost_estimate=pl.CostEstimate(
            flops=4 * count * ncol * BLOCK * BLOCK * width,
            bytes_accessed=4 * count * (ncol * BLOCK + rows) * width,
            transcendentals=0,
        ),
        name="blocks",
    )(tab, occ, vir, *row_shards, *amp_b, *int_b, out)


def gather_cols(amplitudes, integrals, ncol, held):
    arrays, spots = [amplitudes, integrals], {0: ((0, 0), (1, 0))}
    rows = amplitudes.shape[0]
    bit = ncol // 2
    while bit:
        pairs = [(c, c ^ bit) for c in range(ncol)]
        if len(arrays) == 2:
            spots[bit] = ((2, 0), (3, 0))
            arrays.append(lax.ppermute(amplitudes, "col", pairs))
            arrays.append(lax.ppermute(after(integrals, arrays[2]), "col", pairs))
        else:
            starts = np.cumsum([0] + [array.shape[0] // rows for array in arrays])
            moved = {m ^ bit: tuple((len(arrays), int(starts[n]) + q) for n, q in at) for m, at in spots.items()}
            spots.update(moved)
            arrays.append(lax.ppermute(after(jnp.concatenate(arrays), held), "col", pairs))
        bit //= 2
    return arrays, spots


def after(x, gate):
    return x if gate is None else lax.optimization_barrier((x, gate))[0]


def shards(amplitudes, integrals, block_mask, occ_energy, vir_energy):
    nrow = lax.axis_size("row")
    ncol = lax.axis_size("col")
    split = SHARD_BLOCKS
    limit = min(TILES, nrow * ncol)
    where = jnp.stack([lax.axis_index("row"), lax.axis_index("col")]).astype(jnp.int32)
    order = ring_order(nrow)
    spot = {row: at for at, row in enumerate(order)}
    source = np.array([order[(spot[row] - s) % nrow] for row in range(nrow) for s in range(nrow)], np.int32)
    ahead = [(order[p], order[(p + 1) % nrow]) for p in range(nrow)]
    behind = [(b, a) for a, b in ahead]
    tab = slot_table(where, source, block_mask, ncol, nrow, split)
    vir = vir_energy.reshape(-1, BLOCK)
    out = jnp.zeros((limit, BLOCK, BLOCK), jnp.bfloat16)

    def update(hops, amp_b, int_b, out):
        return step(hops, spots, tab, occ_energy, vir, row_shards, amp_b, int_b, out, ncol, nrow, split)

    far = nrow // 2
    amp_up = amp_down = amplitudes
    int_up = int_down = integrals
    for s in range(1, far + 1):
        last = (amp_up, amp_down, int_up, int_down)
        amp_up = lax.ppermute(amp_up, "row", ahead)
        int_down = lax.ppermute(int_down, "row", behind)
        if s < nrow - s:
            int_up = lax.ppermute(int_up, "row", ahead)
            amp_down = lax.ppermute(amp_down, "row", behind)
        if s == min(3, far):
            row_shards, spots = gather_cols(amplitudes, integrals, ncol, (amp_up, int_down, *last))
            out = update((0,), (amplitudes,), (integrals,), out)
            out = update((1, nrow - 1), before[:2], before[2:], out)
        if s >= 3:
            out = update((s - 1, nrow - s + 1), last[:2], last[2:], out)
        before = last
    if far == nrow - far:
        out = update((far,), (amp_up,), (int_down,), out)
    else:
        out = update((far, nrow - far), (amp_up, amp_down), (int_up, int_down), out)
    return out[None, None]


def solution(mesh):
    in_specs = (P(("row", "col"), None), P(("row", "col"), None), P("row", None), P(), P())
    out_specs = P("row", "col", None, None, None)
    return jax.shard_map(shards, mesh=mesh, in_specs=in_specs, out_specs=out_specs, check_vma=False)
```

```python
import functools

import jax
import jax.numpy as jnp
import numpy as np
from jax import lax
from jax.experimental import pallas as pl
from jax.experimental.pallas import tpu as pltpu
from jax.sharding import PartitionSpec as P

BLOCK = 128
SHARD_BLOCKS = 2
TILES = 192


def ring_order(count):
    short = 1
    while short * short * 4 <= count:
        short *= 2
    if count % short or (count // short) % 2 or short == 1:
        return list(range(count))
    tall = count // short
    walk = [z * short for z in range(tall)]
    for at, z in enumerate(reversed(range(tall))):
        xs = range(1, short) if at % 2 == 0 else reversed(range(1, short))
        walk += [z * short + x for x in xs]
    return walk


def table_kernel(ncol, nrow, split, where, source, mask, tab):
    cells = ncol * nrow
    row_at, col_at = where[0], where[1]
    for s in range(nrow):
        tab[3 * cells + s] = source[row_at * nrow + s]
    tab[3 * cells + nrow] = row_at
    tab[3 * cells + nrow + 1] = col_at

    def clear(at, carry):
        tab[at] = -1
        tab[cells + at] = 0
        tab[2 * cells + at] = 0
        return carry

    lax.fori_loop(0, cells, clear, 0)

    def rows(u, count):
        def cols(i, count):
            for trail in range(split):
                hit = mask[u, (i * ncol + col_at) * split + trail] > 0

                @pl.when(hit)
                def _():
                    at = lax.div(u, split) * nrow + i
                    tab[at] = count
                    tab[cells + at] = lax.rem(u, split)
                    tab[2 * cells + at] = trail

                count = count + hit.astype(jnp.int32)
            return count

        return lax.fori_loop(0, nrow, cols, count)

    lax.fori_loop(0, ncol * split, rows, jnp.int32(0))


def slot_table(where, source, mask, ncol, nrow, split):
    smem = pl.BlockSpec(memory_space=pltpu.SMEM)
    return pl.pallas_call(
        functools.partial(table_kernel, ncol, nrow, split),
        in_specs=[smem, smem, smem],
        out_specs=smem,
        out_shape=jax.ShapeDtypeStruct((3 * ncol * nrow + nrow + 2,), jnp.int32),
        name="slots",
    )(where, source, mask)


def step_kernel(hops, ncol, nrow, split, tab, occ, vir, *refs):
    amp_row, int_row = refs[:2]
    refs = refs[2:]
    count = len(hops)
    amp_b, int_b = refs[:count], refs[count : 2 * count]
    _, out, tiles, sem = refs[2 * count :]
    cells = ncol * nrow
    row_at, col_at = tab[3 * cells + nrow], tab[3 * cells + nrow + 1]
    groups = vir.shape[0]
    nt = (((1,), (1,)), ((), ()))

    def half(index):
        return pl.ds(pl.multiple_of(index * BLOCK, BLOCK), BLOCK)

    def gap(block):
        return vir[pl.ds(lax.rem(block, groups), 1), :] - occ[lax.div(block, groups)]

    stores = []
    for n, s in enumerate(hops):
        i = tab[3 * cells + s]
        for j in range(ncol):
            at = j * nrow + i
            lead, trail = tab[cells + at], tab[2 * cells + at]
            a, b = half(j * split + lead), half(trail)
            direct = lax.dot_general(amp_row[a, :], int_b[n][b, :], nt, preferred_element_type=jnp.float32)
            mirror = lax.dot_general(int_row[a, :], amp_b[n][b, :], nt, preferred_element_type=jnp.float32)
            gap_a = gap((row_at * ncol + j) * split + lead)
            gap_b = gap((i * ncol + col_at) * split + trail)
            denom = jnp.broadcast_to(gap_a, (BLOCK, BLOCK)).T + gap_b
            total = direct.astype(jnp.bfloat16).astype(jnp.float32) + mirror.astype(jnp.bfloat16).astype(jnp.float32)
            tiles[n, j] = (total / denom).astype(jnp.bfloat16)
            slot = tab[at]
            stores.append((slot, pltpu.make_async_copy(tiles.at[n, j], out.at[jnp.maximum(slot, 0)], sem.at[n, j])))
    for slot, store in stores:
        pl.when(slot >= 0)(store.start)
    for slot, store in stores:
        pl.when(slot >= 0)(store.wait)


def step(hops, tab, occ, vir, row_shards, amp_b, int_b, out, ncol, nrow, split):
    rows, width = amp_b[0].shape
    count = len(hops)
    smem = pl.BlockSpec(memory_space=pltpu.SMEM)
    vmem = pl.BlockSpec(memory_space=pltpu.VMEM)
    hbm = pl.BlockSpec(memory_space=pl.ANY)
    shard_count = len(row_shards) + 2 * count
    return pl.pallas_call(
        functools.partial(step_kernel, hops, ncol, nrow, split),
        in_specs=[smem, smem, vmem] + [vmem] * shard_count + [hbm],
        out_specs=hbm,
        scratch_shapes=[
            pltpu.VMEM((count, ncol, BLOCK, BLOCK), jnp.bfloat16),
            pltpu.SemaphoreType.DMA((count, ncol)),
        ],
        out_shape=jax.ShapeDtypeStruct(out.shape, out.dtype),
        input_output_aliases={3 + shard_count: 0},
        compiler_params=pltpu.CompilerParams(vmem_limit_bytes=4 * (ncol + count) * rows * width + (4 << 20)),
        cost_estimate=pl.CostEstimate(
            flops=4 * count * ncol * BLOCK * BLOCK * width,
            bytes_accessed=4 * count * (ncol * BLOCK + rows) * width,
            transcendentals=0,
        ),
        name="blocks",
    )(tab, occ, vir, *row_shards, *amp_b, *int_b, out)


def shards(amplitudes, integrals, block_mask, occ_energy, vir_energy):
    nrow = lax.axis_size("row")
    ncol = lax.axis_size("col")
    split = SHARD_BLOCKS
    limit = min(TILES, nrow * ncol)
    where = jnp.stack([lax.axis_index("row"), lax.axis_index("col")]).astype(jnp.int32)
    order = ring_order(nrow)
    spot = {row: at for at, row in enumerate(order)}
    source = np.array([order[(spot[row] - s) % nrow] for row in range(nrow) for s in range(nrow)], np.int32)
    ahead = [(order[p], order[(p + 1) % nrow]) for p in range(nrow)]
    behind = [(b, a) for a, b in ahead]
    tab = slot_table(where, source, block_mask, ncol, nrow, split)
    vir = vir_energy.reshape(-1, BLOCK)
    out = jnp.zeros((limit, BLOCK, BLOCK), jnp.bfloat16)

    row_shards = [lax.all_gather(x, "col", axis=0, tiled=True) for x in (amplitudes, integrals)]

    def update(hops, amp_b, int_b, out):
        return step(hops, tab, occ_energy, vir, row_shards, amp_b, int_b, out, ncol, nrow, split)

    far = nrow // 2
    amp_up = amp_down = amplitudes
    int_up = int_down = integrals
    for s in range(1, far + 1):
        last = (amp_up, amp_down, int_up, int_down)
        amp_up = lax.ppermute(amp_up, "row", ahead)
        int_down = lax.ppermute(int_down, "row", behind)
        if s < nrow - s:
            int_up = lax.ppermute(int_up, "row", ahead)
            amp_down = lax.ppermute(amp_down, "row", behind)
        if s == min(2, far):
            out = update((0,), (amplitudes,), (integrals,), out)
        if s >= 2:
            out = update((s - 1, nrow - s + 1), last[:2], last[2:], out)
    if far == nrow - far:
        out = update((far,), (amp_up,), (int_down,), out)
    else:
        out = update((far, nrow - far), (amp_up, amp_down), (int_up, int_down), out)
    return out[None, None]


def solution(mesh):
    in_specs = (P(("row", "col"), None), P(("row", "col"), None), P("row", None), P(), P())
    out_specs = P("row", "col", None, None, None)
    return jax.shard_map(shards, mesh=mesh, in_specs=in_specs, out_specs=out_specs, check_vma=False)
```

```python
import functools

import jax
import jax.numpy as jnp
import numpy as np
from jax import lax
from jax.experimental import pallas as pl
from jax.experimental.pallas import tpu as pltpu
from jax.sharding import PartitionSpec as P

BLOCK = 128
SHARD_BLOCKS = 2
TILES = 192


def ring_order(count):
    short = 1
    while short * short * 4 <= count:
        short *= 2
    if count % short or (count // short) % 2 or short == 1:
        return list(range(count))
    tall = count // short
    walk = [z * short for z in range(tall)]
    for at, z in enumerate(reversed(range(tall))):
        xs = range(1, short) if at % 2 == 0 else reversed(range(1, short))
        walk += [z * short + x for x in xs]
    return walk


def table_kernel(ncol, nrow, split, where, source, mask, tab):
    cells = ncol * nrow
    row_at, col_at = where[0], where[1]
    for s in range(nrow):
        tab[3 * cells + s] = source[row_at * nrow + s]
    tab[3 * cells + nrow] = row_at
    tab[3 * cells + nrow + 1] = col_at

    def clear(at, carry):
        tab[at] = -1
        tab[cells + at] = 0
        tab[2 * cells + at] = 0
        return carry

    lax.fori_loop(0, cells, clear, 0)

    def rows(u, count):
        def cols(i, count):
            for trail in range(split):
                hit = mask[u, (i * ncol + col_at) * split + trail] > 0

                @pl.when(hit)
                def _():
                    at = lax.div(u, split) * nrow + i
                    tab[at] = count
                    tab[cells + at] = lax.rem(u, split)
                    tab[2 * cells + at] = trail

                count = count + hit.astype(jnp.int32)
            return count

        return lax.fori_loop(0, nrow, cols, count)

    lax.fori_loop(0, ncol * split, rows, jnp.int32(0))


def slot_table(where, source, mask, ncol, nrow, split):
    smem = pl.BlockSpec(memory_space=pltpu.SMEM)
    return pl.pallas_call(
        functools.partial(table_kernel, ncol, nrow, split),
        in_specs=[smem, smem, smem],
        out_specs=smem,
        out_shape=jax.ShapeDtypeStruct((3 * ncol * nrow + nrow + 2,), jnp.int32),
        name="slots",
    )(where, source, mask)


def step_kernel(hops, spots, ncol, nrow, split, tab, occ, vir, *refs):
    kept = 1 + max(n for at in spots.values() for n, _ in at)
    row_shards = refs[:kept]
    refs = refs[kept:]
    count = len(hops)
    rows = split * BLOCK
    amp_b, int_b = refs[:count], refs[count : 2 * count]
    _, out, tiles, sem = refs[2 * count :]
    cells = ncol * nrow
    row_at, col_at = tab[3 * cells + nrow], tab[3 * cells + nrow + 1]
    groups = vir.shape[0]
    nt = (((1,), (1,)), ((), ()))

    def half(index):
        return pl.ds(pl.multiple_of(index * BLOCK, BLOCK), BLOCK)

    def gap(block):
        return vir[pl.ds(lax.rem(block, groups), 1), :] - occ[lax.div(block, groups)]

    stores = []
    for n, s in enumerate(hops):
        i = tab[3 * cells + s]
        for m in range(ncol):
            j = jnp.bitwise_xor(col_at, m)
            at = j * nrow + i
            lead, trail = tab[cells + at], tab[2 * cells + at]
            a, b = half(lead), half(trail)
            amp_a, int_a = (row_shards[n_at].at[pl.ds(q * rows, rows)] for n_at, q in spots[m])
            direct = lax.dot_general(amp_a[a, :], int_b[n][b, :], nt, preferred_element_type=jnp.float32)
            mirror = lax.dot_general(int_a[a, :], amp_b[n][b, :], nt, preferred_element_type=jnp.float32)
            gap_a = gap((row_at * ncol + j) * split + lead)
            gap_b = gap((i * ncol + col_at) * split + trail)
            denom = jnp.broadcast_to(gap_a, (BLOCK, BLOCK)).T + gap_b
            total = direct.astype(jnp.bfloat16).astype(jnp.float32) + mirror.astype(jnp.bfloat16).astype(jnp.float32)
            tiles[n, m] = (total / denom).astype(jnp.bfloat16)
            slot = tab[at]
            stores.append((slot, pltpu.make_async_copy(tiles.at[n, m], out.at[jnp.maximum(slot, 0)], sem.at[n, m])))
    for slot, store in stores:
        pl.when(slot >= 0)(store.start)
    for slot, store in stores:
        pl.when(slot >= 0)(store.wait)


def step(hops, spots, tab, occ, vir, row_shards, amp_b, int_b, out, ncol, nrow, split):
    rows, width = amp_b[0].shape
    count = len(hops)
    smem = pl.BlockSpec(memory_space=pltpu.SMEM)
    vmem = pl.BlockSpec(memory_space=pltpu.VMEM)
    hbm = pl.BlockSpec(memory_space=pl.ANY)
    shard_count = len(row_shards) + 2 * count
    return pl.pallas_call(
        functools.partial(step_kernel, hops, spots, ncol, nrow, split),
        in_specs=[smem, smem, vmem] + [vmem] * shard_count + [hbm],
        out_specs=hbm,
        scratch_shapes=[
            pltpu.VMEM((count, ncol, BLOCK, BLOCK), jnp.bfloat16),
            pltpu.SemaphoreType.DMA((count, ncol)),
        ],
        out_shape=jax.ShapeDtypeStruct(out.shape, out.dtype),
        input_output_aliases={3 + shard_count: 0},
        compiler_params=pltpu.CompilerParams(vmem_limit_bytes=4 * (ncol + count) * rows * width + (4 << 20)),
        cost_estimate=pl.CostEstimate(
            flops=4 * count * ncol * BLOCK * BLOCK * width,
            bytes_accessed=4 * count * (ncol * BLOCK + rows) * width,
            transcendentals=0,
        ),
        name="blocks",
    )(tab, occ, vir, *row_shards, *amp_b, *int_b, out)


def gather_cols(amplitudes, integrals, ncol):
    arrays, spots = [amplitudes, integrals], {0: ((0, 0), (1, 0))}
    bit = ncol // 2
    while bit:
        pairs = [(c, c ^ bit) for c in range(ncol)]
        if len(arrays) == 2:
            spots[bit] = ((2, 0), (3, 0))
            arrays.append(lax.ppermute(amplitudes, "col", pairs))
            arrays.append(lax.ppermute(integrals, "col", pairs))
        else:
            for n, array in enumerate(list(arrays)):
                arrays.append(lax.ppermute(array, "col", pairs))
            known = len(arrays) // 2
            spots.update({m ^ bit: tuple((n + known, q) for n, q in at) for m, at in spots.items()})
        bit //= 2
    return arrays, spots


def shards(amplitudes, integrals, block_mask, occ_energy, vir_energy):
    nrow = lax.axis_size("row")
    ncol = lax.axis_size("col")
    split = SHARD_BLOCKS
    limit = min(TILES, nrow * ncol)
    where = jnp.stack([lax.axis_index("row"), lax.axis_index("col")]).astype(jnp.int32)
    order = ring_order(nrow)
    spot = {row: at for at, row in enumerate(order)}
    source = np.array([order[(spot[row] - s) % nrow] for row in range(nrow) for s in range(nrow)], np.int32)
    ahead = [(order[p], order[(p + 1) % nrow]) for p in range(nrow)]
    behind = [(b, a) for a, b in ahead]
    tab = slot_table(where, source, block_mask, ncol, nrow, split)
    vir = vir_energy.reshape(-1, BLOCK)
    out = jnp.zeros((limit, BLOCK, BLOCK), jnp.bfloat16)

    def update(hops, amp_b, int_b, out):
        return step(hops, spots, tab, occ_energy, vir, row_shards, amp_b, int_b, out, ncol, nrow, split)

    far = nrow // 2
    amp_up = amp_down = amplitudes
    int_up = int_down = integrals
    waiting = []
    for s in range(1, far + 1):
        last = (amp_up, amp_down, int_up, int_down)
        amp_up = lax.ppermute(amp_up, "row", ahead)
        int_down = lax.ppermute(int_down, "row", behind)
        if s < nrow - s:
            int_up = lax.ppermute(int_up, "row", ahead)
            amp_down = lax.ppermute(amp_down, "row", behind)
        if s == min(3, far):
            row_shards, spots = gather_cols(amplitudes, integrals, ncol)
        waiting.append((s - 1, last[0], last[2]))
        if s >= 2:
            waiting.append((nrow - s + 1, last[1], last[3]))
        if s >= min(3, far):
            hops, amp_b, int_b = zip(*waiting)
            out = update(hops, amp_b, int_b, out)
            waiting = []
    if far == nrow - far:
        out = update((far,), (amp_up,), (int_down,), out)
    else:
        out = update((far, nrow - far), (amp_up, amp_down), (int_up, int_down), out)
    return out[None, None]


def solution(mesh):
    in_specs = (P(("row", "col"), None), P(("row", "col"), None), P("row", None), P(), P())
    out_specs = P("row", "col", None, None, None)
    return jax.shard_map(shards, mesh=mesh, in_specs=in_specs, out_specs=out_specs, check_vma=False)
```

```python
import functools

import jax
import jax.numpy as jnp
import numpy as np
from jax import lax
from jax.experimental import pallas as pl
from jax.experimental.pallas import tpu as pltpu
from jax.sharding import PartitionSpec as P

BLOCK = 128
SHARD_BLOCKS = 2
TILES = 192


def ring_order(count):
    short = 1
    while short * short * 4 <= count:
        short *= 2
    if count % short or (count // short) % 2 or short == 1:
        return list(range(count))
    tall = count // short
    walk = [z * short for z in range(tall)]
    for at, z in enumerate(reversed(range(tall))):
        xs = range(1, short) if at % 2 == 0 else reversed(range(1, short))
        walk += [z * short + x for x in xs]
    return walk


def table_kernel(ncol, nrow, split, where, source, mask, tab, empty):
    cells = ncol * nrow
    row_at, col_at = where[0], where[1]
    for s in range(nrow):
        tab[3 * cells + s] = source[row_at * nrow + s]
    tab[3 * cells + nrow] = row_at
    tab[3 * cells + nrow + 1] = col_at

    def clear(at, carry):
        tab[at] = -1
        tab[cells + at] = 0
        tab[2 * cells + at] = 0
        return carry

    lax.fori_loop(0, cells, clear, 0)

    def rows(u, count):
        def cols(i, count):
            for trail in range(split):
                hit = mask[u, (i * ncol + col_at) * split + trail] > 0

                @pl.when(hit)
                def _():
                    at = lax.div(u, split) * nrow + i
                    tab[at] = count
                    tab[cells + at] = lax.rem(u, split)
                    tab[2 * cells + at] = trail

                count = count + hit.astype(jnp.int32)
            return count

        return lax.fori_loop(0, nrow, cols, count)

    lax.fori_loop(0, ncol * split, rows, jnp.int32(0))

    def blank(slot, carry):
        empty[slot] = jnp.zeros((BLOCK, BLOCK), empty.dtype)
        return carry

    lax.fori_loop(0, empty.shape[0], blank, 0)


def slot_table(where, source, mask, ncol, nrow, split, limit):
    smem = pl.BlockSpec(memory_space=pltpu.SMEM)
    return pl.pallas_call(
        functools.partial(table_kernel, ncol, nrow, split),
        in_specs=[smem, smem, smem],
        out_specs=(smem, pl.BlockSpec(memory_space=pltpu.VMEM)),
        out_shape=(
            jax.ShapeDtypeStruct((3 * ncol * nrow + nrow + 2,), jnp.int32),
            jax.ShapeDtypeStruct((limit, BLOCK, BLOCK), jnp.bfloat16),
        ),
        compiler_params=pltpu.CompilerParams(vmem_limit_bytes=2 * limit * BLOCK * BLOCK + (4 << 20)),
        name="slots",
    )(where, source, mask)


def step_kernel(hops, spots, ncol, nrow, split, tab, occ, vir, *refs):
    kept = 1 + max(n for at in spots.values() for n, _ in at)
    row_shards = refs[:kept]
    refs = refs[kept:]
    count = len(hops)
    rows = split * BLOCK
    amp_b, int_b = refs[:count], refs[count : 2 * count]
    _, out, tiles, sem = refs[2 * count :]
    cells = ncol * nrow
    row_at, col_at = tab[3 * cells + nrow], tab[3 * cells + nrow + 1]
    groups = vir.shape[0]
    nt = (((1,), (1,)), ((), ()))

    def half(index):
        return pl.ds(pl.multiple_of(index * BLOCK, BLOCK), BLOCK)

    def gap(block):
        return vir[pl.ds(lax.rem(block, groups), 1), :] - occ[lax.div(block, groups)]

    stores = []
    for n, s in enumerate(hops):
        i = tab[3 * cells + s]
        for m in range(ncol):
            j = jnp.bitwise_xor(col_at, m)
            at = j * nrow + i
            lead, trail = tab[cells + at], tab[2 * cells + at]
            a, b = half(lead), half(trail)
            amp_a, int_a = (row_shards[n_at].at[pl.ds(q * rows, rows)] for n_at, q in spots[m])
            direct = lax.dot_general(amp_a[a, :], int_b[n][b, :], nt, preferred_element_type=jnp.float32)
            mirror = lax.dot_general(int_a[a, :], amp_b[n][b, :], nt, preferred_element_type=jnp.float32)
            gap_a = gap((row_at * ncol + j) * split + lead)
            gap_b = gap((i * ncol + col_at) * split + trail)
            denom = jnp.broadcast_to(gap_a, (BLOCK, BLOCK)).T + gap_b
            total = direct.astype(jnp.bfloat16).astype(jnp.float32) + mirror.astype(jnp.bfloat16).astype(jnp.float32)
            tiles[n, m] = (total / denom).astype(jnp.bfloat16)
            slot = tab[at]
            stores.append((slot, pltpu.make_async_copy(tiles.at[n, m], out.at[jnp.maximum(slot, 0)], sem.at[n, m])))
    for slot, store in stores:
        pl.when(slot >= 0)(store.start)
    for slot, store in stores:
        pl.when(slot >= 0)(store.wait)


def step(hops, spots, tab, occ, vir, row_shards, amp_b, int_b, out, ncol, nrow, split):
    rows, width = amp_b[0].shape
    count = len(hops)
    smem = pl.BlockSpec(memory_space=pltpu.SMEM)
    vmem = pl.BlockSpec(memory_space=pltpu.VMEM)
    hbm = pl.BlockSpec(memory_space=pl.ANY)
    shard_count = len(row_shards) + 2 * count
    return pl.pallas_call(
        functools.partial(step_kernel, hops, spots, ncol, nrow, split),
        in_specs=[smem, smem, vmem] + [vmem] * shard_count + [hbm],
        out_specs=hbm,
        scratch_shapes=[
            pltpu.VMEM((count, ncol, BLOCK, BLOCK), jnp.bfloat16),
            pltpu.SemaphoreType.DMA((count, ncol)),
        ],
        out_shape=jax.ShapeDtypeStruct(out.shape, out.dtype),
        input_output_aliases={3 + shard_count: 0},
        compiler_params=pltpu.CompilerParams(vmem_limit_bytes=4 * (ncol + count) * rows * width + (4 << 20)),
        cost_estimate=pl.CostEstimate(
            flops=4 * count * ncol * BLOCK * BLOCK * width,
            bytes_accessed=4 * count * (ncol * BLOCK + rows) * width,
            transcendentals=0,
        ),
        name="blocks",
    )(tab, occ, vir, *row_shards, *amp_b, *int_b, out)


def gather_cols(amplitudes, integrals, ncol):
    arrays, spots = [amplitudes, integrals], {0: ((0, 0), (1, 0))}
    bit = ncol // 2
    while bit:
        pairs = [(c, c ^ bit) for c in range(ncol)]
        if len(arrays) == 2:
            spots[bit] = ((2, 0), (3, 0))
            arrays.append(lax.ppermute(amplitudes, "col", pairs))
            arrays.append(lax.ppermute(integrals, "col", pairs))
        else:
            for n, array in enumerate(list(arrays)):
                arrays.append(lax.ppermute(array, "col", pairs))
            known = len(arrays) // 2
            spots.update({m ^ bit: tuple((n + known, q) for n, q in at) for m, at in spots.items()})
        bit //= 2
    return arrays, spots


def after(x, gate):
    return x if gate is None else lax.optimization_barrier((x, gate))[0]


def shards(amplitudes, integrals, block_mask, occ_energy, vir_energy):
    nrow = lax.axis_size("row")
    ncol = lax.axis_size("col")
    split = SHARD_BLOCKS
    limit = min(TILES, nrow * ncol)
    where = jnp.stack([lax.axis_index("row"), lax.axis_index("col")]).astype(jnp.int32)
    order = ring_order(nrow)
    spot = {row: at for at, row in enumerate(order)}
    source = np.array([order[(spot[row] - s) % nrow] for row in range(nrow) for s in range(nrow)], np.int32)
    ahead = [(order[p], order[(p + 1) % nrow]) for p in range(nrow)]
    behind = [(b, a) for a, b in ahead]
    tab, out = slot_table(where, source, block_mask, ncol, nrow, split, limit)
    vir = vir_energy.reshape(-1, BLOCK)

    def update(hops, amp_b, int_b, out):
        return step(hops, spots, tab, occ_energy, vir, row_shards, amp_b, int_b, out, ncol, nrow, split)

    far = nrow // 2
    amp_up = amp_down = amplitudes
    int_up = int_down = integrals
    waiting = []
    for s in range(1, far + 1):
        last = (amp_up, amp_down, int_up, int_down)
        gate = tab if s == 2 else None
        amp_up = lax.ppermute(after(amp_up, gate), "row", ahead)
        int_down = lax.ppermute(after(int_down, gate), "row", behind)
        if s < nrow - s:
            int_up = lax.ppermute(int_up, "row", ahead)
            amp_down = lax.ppermute(amp_down, "row", behind)
        if s == min(3, far):
            row_shards, spots = gather_cols(amplitudes, integrals, ncol)
        waiting.append((s - 1, last[0], last[2]))
        if s >= 2:
            waiting.append((nrow - s + 1, last[1], last[3]))
        if s >= min(3, far):
            hops, amp_b, int_b = zip(*waiting)
            out = update(hops, amp_b, int_b, out)
            waiting = []
    if far == nrow - far:
        out = update((far,), (amp_up,), (int_down,), out)
    else:
        out = update((far, nrow - far), (amp_up, amp_down), (int_up, int_down), out)
    return out[None, None]


def solution(mesh):
    in_specs = (P(("row", "col"), None), P(("row", "col"), None), P("row", None), P(), P())
    out_specs = P("row", "col", None, None, None)
    return jax.shard_map(shards, mesh=mesh, in_specs=in_specs, out_specs=out_specs, check_vma=False)
```

```python
import functools

import jax
import jax.numpy as jnp
import numpy as np
from jax import lax
from jax.experimental import pallas as pl
from jax.experimental.pallas import tpu as pltpu
from jax.sharding import PartitionSpec as P

BLOCK = 128
SHARD_BLOCKS = 2
TILES = 192


def ring_order(count):
    short = 1
    while short * short * 4 <= count:
        short *= 2
    if count % short or (count // short) % 2 or short == 1:
        return list(range(count))
    tall = count // short
    walk = [z * short for z in range(tall)]
    for at, z in enumerate(reversed(range(tall))):
        xs = range(1, short) if at % 2 == 0 else reversed(range(1, short))
        walk += [z * short + x for x in xs]
    return walk


def table_kernel(ncol, nrow, split, where, source, mask, tab, empty):
    cells = ncol * nrow
    row_at, col_at = where[0], where[1]
    for s in range(nrow):
        tab[3 * cells + s] = source[row_at * nrow + s]
    tab[3 * cells + nrow] = row_at
    tab[3 * cells + nrow + 1] = col_at

    def clear(at, carry):
        tab[at] = -1
        tab[cells + at] = 0
        tab[2 * cells + at] = 0
        return carry

    lax.fori_loop(0, cells, clear, 0)

    def rows(u, count):
        def cols(i, count):
            for trail in range(split):
                hit = mask[u, (i * ncol + col_at) * split + trail] > 0

                @pl.when(hit)
                def _():
                    at = lax.div(u, split) * nrow + i
                    tab[at] = count
                    tab[cells + at] = lax.rem(u, split)
                    tab[2 * cells + at] = trail

                count = count + hit.astype(jnp.int32)
            return count

        return lax.fori_loop(0, nrow, cols, count)

    lax.fori_loop(0, ncol * split, rows, jnp.int32(0))

    def blank(slot, carry):
        empty[slot] = jnp.zeros((BLOCK, BLOCK), empty.dtype)
        return carry

    lax.fori_loop(0, empty.shape[0], blank, 0)


def slot_table(where, source, mask, ncol, nrow, split, limit):
    smem = pl.BlockSpec(memory_space=pltpu.SMEM)
    return pl.pallas_call(
        functools.partial(table_kernel, ncol, nrow, split),
        in_specs=[smem, smem, smem],
        out_specs=(smem, pl.BlockSpec(memory_space=pltpu.VMEM)),
        out_shape=(
            jax.ShapeDtypeStruct((3 * ncol * nrow + nrow + 2,), jnp.int32),
            jax.ShapeDtypeStruct((limit, BLOCK, BLOCK), jnp.bfloat16),
        ),
        compiler_params=pltpu.CompilerParams(vmem_limit_bytes=2 * limit * BLOCK * BLOCK + (4 << 20)),
        name="slots",
    )(where, source, mask)


def step_kernel(hops, spots, ncol, nrow, split, tab, occ, vir, *refs):
    kept = 1 + max(n for at in spots.values() for n, _ in at)
    row_shards = refs[:kept]
    refs = refs[kept:]
    count = len(hops)
    rows = split * BLOCK
    amp_b, int_b = refs[:count], refs[count : 2 * count]
    _, out, tiles, sem = refs[2 * count :]
    cells = ncol * nrow
    row_at, col_at = tab[3 * cells + nrow], tab[3 * cells + nrow + 1]
    groups = vir.shape[0]
    nt = (((1,), (1,)), ((), ()))

    def half(index):
        return pl.ds(pl.multiple_of(index * BLOCK, BLOCK), BLOCK)

    def gap(block):
        return vir[pl.ds(lax.rem(block, groups), 1), :] - occ[lax.div(block, groups)]

    stores = []
    for n, s in enumerate(hops):
        i = tab[3 * cells + s]
        for m in range(ncol):
            j = jnp.bitwise_xor(col_at, m)
            at = j * nrow + i
            lead, trail = tab[cells + at], tab[2 * cells + at]
            a, b = half(lead), half(trail)
            amp_a, int_a = (row_shards[n_at].at[pl.ds(q * rows, rows)] for n_at, q in spots[m])
            direct = lax.dot_general(amp_a[a, :], int_b[n][b, :], nt, preferred_element_type=jnp.float32)
            mirror = lax.dot_general(int_a[a, :], amp_b[n][b, :], nt, preferred_element_type=jnp.float32)
            gap_a = gap((row_at * ncol + j) * split + lead)
            gap_b = gap((i * ncol + col_at) * split + trail)
            denom = jnp.broadcast_to(gap_a, (BLOCK, BLOCK)).T + gap_b
            total = direct.astype(jnp.bfloat16).astype(jnp.float32) + mirror.astype(jnp.bfloat16).astype(jnp.float32)
            tiles[n, m] = (total / denom).astype(jnp.bfloat16)
            slot = tab[at]
            stores.append((slot, pltpu.make_async_copy(tiles.at[n, m], out.at[jnp.maximum(slot, 0)], sem.at[n, m])))
    for slot, store in stores:
        pl.when(slot >= 0)(store.start)
    for slot, store in stores:
        pl.when(slot >= 0)(store.wait)


def step(hops, spots, tab, occ, vir, row_shards, amp_b, int_b, out, ncol, nrow, split):
    rows, width = amp_b[0].shape
    count = len(hops)
    smem = pl.BlockSpec(memory_space=pltpu.SMEM)
    vmem = pl.BlockSpec(memory_space=pltpu.VMEM)
    hbm = pl.BlockSpec(memory_space=pl.ANY)
    shard_count = len(row_shards) + 2 * count
    return pl.pallas_call(
        functools.partial(step_kernel, hops, spots, ncol, nrow, split),
        in_specs=[smem, smem, vmem] + [vmem] * shard_count + [hbm],
        out_specs=hbm,
        scratch_shapes=[
            pltpu.VMEM((count, ncol, BLOCK, BLOCK), jnp.bfloat16),
            pltpu.SemaphoreType.DMA((count, ncol)),
        ],
        out_shape=jax.ShapeDtypeStruct(out.shape, out.dtype),
        input_output_aliases={3 + shard_count: 0},
        compiler_params=pltpu.CompilerParams(vmem_limit_bytes=4 * (ncol + count) * rows * width + (4 << 20)),
        cost_estimate=pl.CostEstimate(
            flops=4 * count * ncol * BLOCK * BLOCK * width,
            bytes_accessed=4 * count * (ncol * BLOCK + rows) * width,
            transcendentals=0,
        ),
        name="blocks",
    )(tab, occ, vir, *row_shards, *amp_b, *int_b, out)


def gather_cols(amplitudes, integrals, ncol):
    arrays, spots = [amplitudes, integrals], {0: ((0, 0), (1, 0))}
    bit = ncol // 2
    while bit:
        pairs = [(c, c ^ bit) for c in range(ncol)]
        if len(arrays) == 2:
            spots[bit] = ((2, 0), (3, 0))
            arrays.append(lax.ppermute(amplitudes, "col", pairs))
            arrays.append(lax.ppermute(after(integrals, arrays[2]), "col", pairs))
        else:
            for n, array in enumerate(list(arrays)):
                arrays.append(lax.ppermute(array, "col", pairs))
            known = len(arrays) // 2
            spots.update({m ^ bit: tuple((n + known, q) for n, q in at) for m, at in spots.items()})
        bit //= 2
    return arrays, spots


def after(x, gate):
    return x if gate is None else lax.optimization_barrier((x, gate))[0]


def shards(amplitudes, integrals, block_mask, occ_energy, vir_energy):
    nrow = lax.axis_size("row")
    ncol = lax.axis_size("col")
    split = SHARD_BLOCKS
    limit = min(TILES, nrow * ncol)
    where = jnp.stack([lax.axis_index("row"), lax.axis_index("col")]).astype(jnp.int32)
    order = ring_order(nrow)
    spot = {row: at for at, row in enumerate(order)}
    source = np.array([order[(spot[row] - s) % nrow] for row in range(nrow) for s in range(nrow)], np.int32)
    ahead = [(order[p], order[(p + 1) % nrow]) for p in range(nrow)]
    behind = [(b, a) for a, b in ahead]
    tab, out = slot_table(where, source, block_mask, ncol, nrow, split, limit)
    vir = vir_energy.reshape(-1, BLOCK)

    def update(hops, amp_b, int_b, out):
        return step(hops, spots, tab, occ_energy, vir, row_shards, amp_b, int_b, out, ncol, nrow, split)

    far = nrow // 2
    amp_up = amp_down = amplitudes
    int_up = int_down = integrals
    waiting = []
    for s in range(1, far + 1):
        last = (amp_up, amp_down, int_up, int_down)
        gate = tab if s == 2 else None
        amp_up = lax.ppermute(after(amp_up, gate), "row", ahead)
        int_down = lax.ppermute(after(int_down, gate), "row", behind)
        if s < nrow - s:
            int_up = lax.ppermute(int_up, "row", ahead)
            amp_down = lax.ppermute(amp_down, "row", behind)
        if s == min(3, far):
            row_shards, spots = gather_cols(amplitudes, integrals, ncol)
        waiting.append((s - 1, last[0], last[2]))
        if s >= 2:
            waiting.append((nrow - s + 1, last[1], last[3]))
        if s >= min(3, far):
            hops, amp_b, int_b = zip(*waiting)
            out = update(hops, amp_b, int_b, out)
            waiting = []
    if far == nrow - far:
        out = update((far,), (amp_up,), (int_down,), out)
    else:
        out = update((far, nrow - far), (amp_up, amp_down), (int_up, int_down), out)
    return out[None, None]


def solution(mesh):
    in_specs = (P(("row", "col"), None), P(("row", "col"), None), P("row", None), P(), P())
    out_specs = P("row", "col", None, None, None)
    return jax.shard_map(shards, mesh=mesh, in_specs=in_specs, out_specs=out_specs, check_vma=False)
```

```python
import functools

import jax
import jax.numpy as jnp
import numpy as np
from jax import lax
from jax.experimental import pallas as pl
from jax.experimental.pallas import tpu as pltpu
from jax.sharding import PartitionSpec as P

BLOCK = 128
SHARD_BLOCKS = 2
TILES = 192


def ring_order(count):
    short = 1
    while short * short * 4 <= count:
        short *= 2
    if count % short or (count // short) % 2 or short == 1:
        return list(range(count))
    tall = count // short
    walk = [z * short for z in range(tall)]
    for at, z in enumerate(reversed(range(tall))):
        xs = range(1, short) if at % 2 == 0 else reversed(range(1, short))
        walk += [z * short + x for x in xs]
    return walk


def table_kernel(ncol, nrow, split, where, source, mask, tab, empty):
    cells = ncol * nrow
    row_at, col_at = where[0], where[1]
    for s in range(nrow):
        tab[3 * cells + s] = source[row_at * nrow + s]
    tab[3 * cells + nrow] = row_at
    tab[3 * cells + nrow + 1] = col_at

    def clear(at, carry):
        tab[at] = -1
        tab[cells + at] = 0
        tab[2 * cells + at] = 0
        return carry

    lax.fori_loop(0, cells, clear, 0)

    def rows(u, count):
        def cols(i, count):
            for trail in range(split):
                hit = mask[u, (i * ncol + col_at) * split + trail] > 0

                @pl.when(hit)
                def _():
                    at = lax.div(u, split) * nrow + i
                    tab[at] = count
                    tab[cells + at] = lax.rem(u, split)
                    tab[2 * cells + at] = trail

                count = count + hit.astype(jnp.int32)
            return count

        return lax.fori_loop(0, nrow, cols, count)

    lax.fori_loop(0, ncol * split, rows, jnp.int32(0))

    def blank(slot, carry):
        empty[slot] = jnp.zeros((BLOCK, BLOCK), empty.dtype)
        return carry

    lax.fori_loop(0, empty.shape[0], blank, 0)


def slot_table(where, source, mask, ncol, nrow, split, limit):
    smem = pl.BlockSpec(memory_space=pltpu.SMEM)
    return pl.pallas_call(
        functools.partial(table_kernel, ncol, nrow, split),
        in_specs=[smem, smem, smem],
        out_specs=(smem, pl.BlockSpec(memory_space=pltpu.VMEM)),
        out_shape=(
            jax.ShapeDtypeStruct((3 * ncol * nrow + nrow + 2,), jnp.int32),
            jax.ShapeDtypeStruct((limit, BLOCK, BLOCK), jnp.bfloat16),
        ),
        compiler_params=pltpu.CompilerParams(vmem_limit_bytes=2 * limit * BLOCK * BLOCK + (4 << 20)),
        name="slots",
    )(where, source, mask)


def step_kernel(hops, spots, ncol, nrow, split, tab, occ, vir, *refs):
    kept = 1 + max(n for at in spots.values() for n, _ in at)
    row_shards = refs[:kept]
    refs = refs[kept:]
    count = len(hops)
    rows = split * BLOCK
    amp_b, int_b = refs[:count], refs[count : 2 * count]
    _, out, tiles, sem = refs[2 * count :]
    cells = ncol * nrow
    row_at, col_at = tab[3 * cells + nrow], tab[3 * cells + nrow + 1]
    groups = vir.shape[0]
    nt = (((1,), (1,)), ((), ()))

    def half(index):
        return pl.ds(pl.multiple_of(index * BLOCK, BLOCK), BLOCK)

    def gap(block):
        return vir[pl.ds(lax.rem(block, groups), 1), :] - occ[lax.div(block, groups)]

    stores = []
    for n, s in enumerate(hops):
        i = tab[3 * cells + s]
        for m in range(ncol):
            j = jnp.bitwise_xor(col_at, m)
            at = j * nrow + i
            lead, trail = tab[cells + at], tab[2 * cells + at]
            a, b = half(lead), half(trail)
            amp_a, int_a = (row_shards[n_at].at[pl.ds(q * rows, rows)] for n_at, q in spots[m])
            direct = lax.dot_general(amp_a[a, :], int_b[n][b, :], nt, preferred_element_type=jnp.float32)
            mirror = lax.dot_general(int_a[a, :], amp_b[n][b, :], nt, preferred_element_type=jnp.float32)
            gap_a = gap((row_at * ncol + j) * split + lead)
            gap_b = gap((i * ncol + col_at) * split + trail)
            denom = jnp.broadcast_to(gap_a, (BLOCK, BLOCK)).T + gap_b
            total = direct.astype(jnp.bfloat16).astype(jnp.float32) + mirror.astype(jnp.bfloat16).astype(jnp.float32)
            tiles[n, m] = (total / denom).astype(jnp.bfloat16)
            slot = tab[at]
            stores.append((slot, pltpu.make_async_copy(tiles.at[n, m], out.at[jnp.maximum(slot, 0)], sem.at[n, m])))
    for slot, store in stores:
        pl.when(slot >= 0)(store.start)
    for slot, store in stores:
        pl.when(slot >= 0)(store.wait)


def step(hops, spots, tab, occ, vir, row_shards, amp_b, int_b, out, ncol, nrow, split):
    rows, width = amp_b[0].shape
    count = len(hops)
    smem = pl.BlockSpec(memory_space=pltpu.SMEM)
    vmem = pl.BlockSpec(memory_space=pltpu.VMEM)
    hbm = pl.BlockSpec(memory_space=pl.ANY)
    shard_count = len(row_shards) + 2 * count
    return pl.pallas_call(
        functools.partial(step_kernel, hops, spots, ncol, nrow, split),
        in_specs=[smem, smem, vmem] + [vmem] * shard_count + [hbm],
        out_specs=hbm,
        scratch_shapes=[
            pltpu.VMEM((count, ncol, BLOCK, BLOCK), jnp.bfloat16),
            pltpu.SemaphoreType.DMA((count, ncol)),
        ],
        out_shape=jax.ShapeDtypeStruct(out.shape, out.dtype),
        input_output_aliases={3 + shard_count: 0},
        compiler_params=pltpu.CompilerParams(vmem_limit_bytes=4 * (ncol + count) * rows * width + (4 << 20)),
        cost_estimate=pl.CostEstimate(
            flops=4 * count * ncol * BLOCK * BLOCK * width,
            bytes_accessed=4 * count * (ncol * BLOCK + rows) * width,
            transcendentals=0,
        ),
        name="blocks",
    )(tab, occ, vir, *row_shards, *amp_b, *int_b, out)


def gather_cols(amplitudes, integrals, ncol, held):
    arrays, spots = [amplitudes, integrals], {0: ((0, 0), (1, 0))}
    bit = ncol // 2
    while bit:
        pairs = [(c, c ^ bit) for c in range(ncol)]
        if len(arrays) == 2:
            spots[bit] = ((2, 0), (3, 0))
            arrays.append(lax.ppermute(amplitudes, "col", pairs))
            arrays.append(lax.ppermute(after(integrals, arrays[2]), "col", pairs))
        else:
            known = len(arrays)
            for n, array in enumerate(list(arrays)):
                gate = held if n == 0 else arrays[known] if n == 1 else None
                arrays.append(lax.ppermute(after(array, gate), "col", pairs))
            spots.update({m ^ bit: tuple((n + known, q) for n, q in at) for m, at in spots.items()})
        bit //= 2
    return arrays, spots


def after(x, gate):
    return x if gate is None else lax.optimization_barrier((x, gate))[0]


def shards(amplitudes, integrals, block_mask, occ_energy, vir_energy):
    nrow = lax.axis_size("row")
    ncol = lax.axis_size("col")
    split = SHARD_BLOCKS
    limit = min(TILES, nrow * ncol)
    where = jnp.stack([lax.axis_index("row"), lax.axis_index("col")]).astype(jnp.int32)
    order = ring_order(nrow)
    spot = {row: at for at, row in enumerate(order)}
    source = np.array([order[(spot[row] - s) % nrow] for row in range(nrow) for s in range(nrow)], np.int32)
    ahead = [(order[p], order[(p + 1) % nrow]) for p in range(nrow)]
    behind = [(b, a) for a, b in ahead]
    tab, out = slot_table(where, source, block_mask, ncol, nrow, split, limit)
    vir = vir_energy.reshape(-1, BLOCK)

    def update(hops, amp_b, int_b, out):
        return step(hops, spots, tab, occ_energy, vir, row_shards, amp_b, int_b, out, ncol, nrow, split)

    far = nrow // 2
    amp_up = amp_down = amplitudes
    int_up = int_down = integrals
    waiting, held = [], None
    for s in range(1, far + 1):
        held = (amp_up, int_down) if s == 2 else held
        last = (amp_up, amp_down, int_up, int_down)
        gate = tab if s == 2 else None
        amp_up = lax.ppermute(after(amp_up, gate), "row", ahead)
        int_down = lax.ppermute(after(int_down, gate), "row", behind)
        if s < nrow - s:
            int_up = lax.ppermute(int_up, "row", ahead)
            amp_down = lax.ppermute(amp_down, "row", behind)
        if s == min(3, far):
            row_shards, spots = gather_cols(amplitudes, integrals, ncol, held)
        waiting.append((s - 1, last[0], last[2]))
        if s >= 2:
            waiting.append((nrow - s + 1, last[1], last[3]))
        if s >= min(3, far):
            hops, amp_b, int_b = zip(*waiting)
            out = update(hops, amp_b, int_b, out)
            waiting = []
    if far == nrow - far:
        out = update((far,), (amp_up,), (int_down,), out)
    else:
        out = update((far, nrow - far), (amp_up, amp_down), (int_up, int_down), out)
    return out[None, None]


def solution(mesh):
    in_specs = (P(("row", "col"), None), P(("row", "col"), None), P("row", None), P(), P())
    out_specs = P("row", "col", None, None, None)
    return jax.shard_map(shards, mesh=mesh, in_specs=in_specs, out_specs=out_specs, check_vma=False)
```

```python
import functools

import jax
import jax.numpy as jnp
import numpy as np
from jax import lax
from jax.experimental import pallas as pl
from jax.experimental.pallas import tpu as pltpu
from jax.sharding import PartitionSpec as P

BLOCK = 128
SHARD_BLOCKS = 2
TILES = 192


def ring_order(count):
    short = 1
    while short * short * 4 <= count:
        short *= 2
    if count % short or (count // short) % 2 or short == 1:
        return list(range(count))
    tall = count // short
    walk = [z * short for z in range(tall)]
    for at, z in enumerate(reversed(range(tall))):
        xs = range(1, short) if at % 2 == 0 else reversed(range(1, short))
        walk += [z * short + x for x in xs]
    return walk


def table_kernel(ncol, nrow, split, where, source, mask, tab, empty):
    cells = ncol * nrow
    row_at, col_at = where[0], where[1]
    for s in range(nrow):
        tab[3 * cells + s] = source[row_at * nrow + s]
    tab[3 * cells + nrow] = row_at
    tab[3 * cells + nrow + 1] = col_at

    def clear(at, carry):
        tab[at] = -1
        tab[cells + at] = 0
        tab[2 * cells + at] = 0
        return carry

    lax.fori_loop(0, cells, clear, 0)

    def rows(u, count):
        def cols(i, count):
            for trail in range(split):
                hit = mask[u, (i * ncol + col_at) * split + trail] > 0

                @pl.when(hit)
                def _():
                    at = lax.div(u, split) * nrow + i
                    tab[at] = count
                    tab[cells + at] = lax.rem(u, split)
                    tab[2 * cells + at] = trail

                count = count + hit.astype(jnp.int32)
            return count

        return lax.fori_loop(0, nrow, cols, count)

    lax.fori_loop(0, ncol * split, rows, jnp.int32(0))

    def blank(slot, carry):
        empty[slot] = jnp.zeros((BLOCK, BLOCK), empty.dtype)
        return carry

    lax.fori_loop(0, empty.shape[0], blank, 0)


def slot_table(where, source, mask, ncol, nrow, split, limit):
    smem = pl.BlockSpec(memory_space=pltpu.SMEM)
    return pl.pallas_call(
        functools.partial(table_kernel, ncol, nrow, split),
        in_specs=[smem, smem, smem],
        out_specs=(smem, pl.BlockSpec(memory_space=pltpu.VMEM)),
        out_shape=(
            jax.ShapeDtypeStruct((3 * ncol * nrow + nrow + 2,), jnp.int32),
            jax.ShapeDtypeStruct((limit, BLOCK, BLOCK), jnp.bfloat16),
        ),
        compiler_params=pltpu.CompilerParams(vmem_limit_bytes=2 * limit * BLOCK * BLOCK + (4 << 20)),
        name="slots",
    )(where, source, mask)


def step_kernel(hops, spots, ncol, nrow, split, tab, occ, vir, *refs):
    kept = 1 + max(n for at in spots.values() for n, _ in at)
    row_shards = refs[:kept]
    refs = refs[kept:]
    count = len(hops)
    rows = split * BLOCK
    amp_b, int_b = refs[:count], refs[count : 2 * count]
    _, out, tiles, sem = refs[2 * count :]
    cells = ncol * nrow
    row_at, col_at = tab[3 * cells + nrow], tab[3 * cells + nrow + 1]
    groups = vir.shape[0]
    nt = (((1,), (1,)), ((), ()))

    def half(index):
        return pl.ds(pl.multiple_of(index * BLOCK, BLOCK), BLOCK)

    def gap(block):
        return vir[pl.ds(lax.rem(block, groups), 1), :] - occ[lax.div(block, groups)]

    stores = []
    for n, s in enumerate(hops):
        i = tab[3 * cells + s]
        for m in range(ncol):
            j = jnp.bitwise_xor(col_at, m)
            at = j * nrow + i
            lead, trail = tab[cells + at], tab[2 * cells + at]
            a, b = half(lead), half(trail)
            amp_a, int_a = (row_shards[n_at].at[pl.ds(q * rows, rows)] for n_at, q in spots[m])
            direct = lax.dot_general(amp_a[a, :], int_b[n][b, :], nt, preferred_element_type=jnp.float32)
            mirror = lax.dot_general(int_a[a, :], amp_b[n][b, :], nt, preferred_element_type=jnp.float32)
            gap_a = gap((row_at * ncol + j) * split + lead)
            gap_b = gap((i * ncol + col_at) * split + trail)
            denom = jnp.broadcast_to(gap_a, (BLOCK, BLOCK)).T + gap_b
            total = direct.astype(jnp.bfloat16).astype(jnp.float32) + mirror.astype(jnp.bfloat16).astype(jnp.float32)
            tiles[n, m] = (total / denom).astype(jnp.bfloat16)
            slot = tab[at]
            stores.append((slot, pltpu.make_async_copy(tiles.at[n, m], out.at[jnp.maximum(slot, 0)], sem.at[n, m])))
    for slot, store in stores:
        pl.when(slot >= 0)(store.start)
    for slot, store in stores:
        pl.when(slot >= 0)(store.wait)


def step(hops, spots, tab, occ, vir, row_shards, amp_b, int_b, out, ncol, nrow, split):
    rows, width = amp_b[0].shape
    count = len(hops)
    smem = pl.BlockSpec(memory_space=pltpu.SMEM)
    vmem = pl.BlockSpec(memory_space=pltpu.VMEM)
    hbm = pl.BlockSpec(memory_space=pl.ANY)
    shard_count = len(row_shards) + 2 * count
    return pl.pallas_call(
        functools.partial(step_kernel, hops, spots, ncol, nrow, split),
        in_specs=[smem, smem, vmem] + [vmem] * shard_count + [hbm],
        out_specs=hbm,
        scratch_shapes=[
            pltpu.VMEM((count, ncol, BLOCK, BLOCK), jnp.bfloat16),
            pltpu.SemaphoreType.DMA((count, ncol)),
        ],
        out_shape=jax.ShapeDtypeStruct(out.shape, out.dtype),
        input_output_aliases={3 + shard_count: 0},
        compiler_params=pltpu.CompilerParams(vmem_limit_bytes=4 * (ncol + count) * rows * width + (4 << 20)),
        cost_estimate=pl.CostEstimate(
            flops=4 * count * ncol * BLOCK * BLOCK * width,
            bytes_accessed=4 * count * (ncol * BLOCK + rows) * width,
            transcendentals=0,
        ),
        name="blocks",
    )(tab, occ, vir, *row_shards, *amp_b, *int_b, out)


def gather_cols(amplitudes, integrals, ncol, held):
    arrays, spots = [amplitudes, integrals], {0: ((0, 0), (1, 0))}
    bit = ncol // 2
    while bit:
        pairs = [(c, c ^ bit) for c in range(ncol)]
        if len(arrays) == 2:
            spots[bit] = ((2, 0), (3, 0))
            arrays.append(lax.ppermute(amplitudes, "col", pairs))
            arrays.append(lax.ppermute(after(integrals, arrays[2]), "col", pairs))
        else:
            known = len(arrays)
            for n, array in enumerate(list(arrays)):
                gate = held if n == 1 else None
                arrays.append(lax.ppermute(after(array, gate), "col", pairs))
            spots.update({m ^ bit: tuple((n + known, q) for n, q in at) for m, at in spots.items()})
        bit //= 2
    return arrays, spots


def after(x, gate):
    return x if gate is None else lax.optimization_barrier((x, gate))[0]


def shards(amplitudes, integrals, block_mask, occ_energy, vir_energy):
    nrow = lax.axis_size("row")
    ncol = lax.axis_size("col")
    split = SHARD_BLOCKS
    limit = min(TILES, nrow * ncol)
    where = jnp.stack([lax.axis_index("row"), lax.axis_index("col")]).astype(jnp.int32)
    order = ring_order(nrow)
    spot = {row: at for at, row in enumerate(order)}
    source = np.array([order[(spot[row] - s) % nrow] for row in range(nrow) for s in range(nrow)], np.int32)
    ahead = [(order[p], order[(p + 1) % nrow]) for p in range(nrow)]
    behind = [(b, a) for a, b in ahead]
    tab, out = slot_table(where, source, block_mask, ncol, nrow, split, limit)
    vir = vir_energy.reshape(-1, BLOCK)

    def update(hops, amp_b, int_b, out):
        return step(hops, spots, tab, occ_energy, vir, row_shards, amp_b, int_b, out, ncol, nrow, split)

    far = nrow // 2
    amp_up = amp_down = amplitudes
    int_up = int_down = integrals
    waiting, held = [], None
    for s in range(1, far + 1):
        held = (amp_down,) if s == 2 else held
        last = (amp_up, amp_down, int_up, int_down)
        gate = tab if s == 2 else None
        amp_up = lax.ppermute(after(amp_up, gate), "row", ahead)
        int_down = lax.ppermute(after(int_down, gate), "row", behind)
        if s < nrow - s:
            int_up = lax.ppermute(int_up, "row", ahead)
            amp_down = lax.ppermute(amp_down, "row", behind)
        if s == min(3, far):
            row_shards, spots = gather_cols(amplitudes, integrals, ncol, held)
        waiting.append((s - 1, last[0], last[2]))
        if s >= 2:
            waiting.append((nrow - s + 1, last[1], last[3]))
        if s >= min(3, far):
            hops, amp_b, int_b = zip(*waiting)
            out = update(hops, amp_b, int_b, out)
            waiting = []
    if far == nrow - far:
        out = update((far,), (amp_up,), (int_down,), out)
    else:
        out = update((far, nrow - far), (amp_up, amp_down), (int_up, int_down), out)
    return out[None, None]


def solution(mesh):
    in_specs = (P(("row", "col"), None), P(("row", "col"), None), P("row", None), P(), P())
    out_specs = P("row", "col", None, None, None)
    return jax.shard_map(shards, mesh=mesh, in_specs=in_specs, out_specs=out_specs, check_vma=False)
```

```python
import functools

import jax
import jax.numpy as jnp
import numpy as np
from jax import lax
from jax.experimental import pallas as pl
from jax.experimental.pallas import tpu as pltpu
from jax.sharding import PartitionSpec as P

BLOCK = 128
SHARD_BLOCKS = 2
TILES = 192


def ring_order(count):
    short = 1
    while short * short * 4 <= count:
        short *= 2
    if count % short or (count // short) % 2 or short == 1:
        return list(range(count))
    tall = count // short
    walk = [z * short for z in range(tall)]
    for at, z in enumerate(reversed(range(tall))):
        xs = range(1, short) if at % 2 == 0 else reversed(range(1, short))
        walk += [z * short + x for x in xs]
    return walk


def table_kernel(ncol, nrow, split, where, source, mask, tab, empty):
    cells = ncol * nrow
    row_at, col_at = where[0], where[1]
    for s in range(nrow):
        tab[3 * cells + s] = source[row_at * nrow + s]
    tab[3 * cells + nrow] = row_at
    tab[3 * cells + nrow + 1] = col_at

    def clear(at, carry):
        tab[at] = -1
        tab[cells + at] = 0
        tab[2 * cells + at] = 0
        return carry

    lax.fori_loop(0, cells, clear, 0)

    def rows(u, count):
        def cols(i, count):
            for trail in range(split):
                hit = mask[u, (i * ncol + col_at) * split + trail] > 0

                @pl.when(hit)
                def _():
                    at = lax.div(u, split) * nrow + i
                    tab[at] = count
                    tab[cells + at] = lax.rem(u, split)
                    tab[2 * cells + at] = trail

                count = count + hit.astype(jnp.int32)
            return count

        return lax.fori_loop(0, nrow, cols, count)

    lax.fori_loop(0, ncol * split, rows, jnp.int32(0))

    def blank(slot, carry):
        empty[slot] = jnp.zeros((BLOCK, BLOCK), empty.dtype)
        return carry

    lax.fori_loop(0, empty.shape[0], blank, 0)


def slot_table(where, source, mask, ncol, nrow, split, limit):
    smem = pl.BlockSpec(memory_space=pltpu.SMEM)
    return pl.pallas_call(
        functools.partial(table_kernel, ncol, nrow, split),
        in_specs=[smem, smem, smem],
        out_specs=(smem, pl.BlockSpec(memory_space=pltpu.VMEM)),
        out_shape=(
            jax.ShapeDtypeStruct((3 * ncol * nrow + nrow + 2,), jnp.int32),
            jax.ShapeDtypeStruct((limit, BLOCK, BLOCK), jnp.bfloat16),
        ),
        compiler_params=pltpu.CompilerParams(vmem_limit_bytes=2 * limit * BLOCK * BLOCK + (4 << 20)),
        name="slots",
    )(where, source, mask)


def step_kernel(hops, spots, ncol, nrow, split, tab, occ, vir, *refs):
    kept = 1 + max(n for at in spots.values() for n, _ in at)
    row_shards = refs[:kept]
    refs = refs[kept:]
    count = len(hops)
    rows = split * BLOCK
    amp_b, int_b = refs[:count], refs[count : 2 * count]
    _, out, tiles, sem = refs[2 * count :]
    cells = ncol * nrow
    row_at, col_at = tab[3 * cells + nrow], tab[3 * cells + nrow + 1]
    groups = vir.shape[0]
    nt = (((1,), (1,)), ((), ()))

    def half(index):
        return pl.ds(pl.multiple_of(index * BLOCK, BLOCK), BLOCK)

    def gap(block):
        return vir[pl.ds(lax.rem(block, groups), 1), :] - occ[lax.div(block, groups)]

    stores = []
    for n, s in enumerate(hops):
        i = tab[3 * cells + s]
        for m in range(ncol):
            j = jnp.bitwise_xor(col_at, m)
            at = j * nrow + i
            lead, trail = tab[cells + at], tab[2 * cells + at]
            a, b = half(lead), half(trail)
            amp_a, int_a = (row_shards[n_at].at[pl.ds(q * rows, rows)] for n_at, q in spots[m])
            direct = lax.dot_general(amp_a[a, :], int_b[n][b, :], nt, preferred_element_type=jnp.float32)
            mirror = lax.dot_general(int_a[a, :], amp_b[n][b, :], nt, preferred_element_type=jnp.float32)
            gap_a = gap((row_at * ncol + j) * split + lead)
            gap_b = gap((i * ncol + col_at) * split + trail)
            denom = jnp.broadcast_to(gap_a, (BLOCK, BLOCK)).T + gap_b
            total = direct.astype(jnp.bfloat16).astype(jnp.float32) + mirror.astype(jnp.bfloat16).astype(jnp.float32)
            tiles[n, m] = (total / denom).astype(jnp.bfloat16)
            slot = tab[at]
            stores.append((slot, pltpu.make_async_copy(tiles.at[n, m], out.at[jnp.maximum(slot, 0)], sem.at[n, m])))
    for slot, store in stores:
        pl.when(slot >= 0)(store.start)
    for slot, store in stores:
        pl.when(slot >= 0)(store.wait)


def step(hops, spots, tab, occ, vir, row_shards, amp_b, int_b, out, ncol, nrow, split):
    rows, width = amp_b[0].shape
    count = len(hops)
    smem = pl.BlockSpec(memory_space=pltpu.SMEM)
    vmem = pl.BlockSpec(memory_space=pltpu.VMEM)
    hbm = pl.BlockSpec(memory_space=pl.ANY)
    shard_count = len(row_shards) + 2 * count
    return pl.pallas_call(
        functools.partial(step_kernel, hops, spots, ncol, nrow, split),
        in_specs=[smem, smem, vmem] + [vmem] * shard_count + [hbm],
        out_specs=hbm,
        scratch_shapes=[
            pltpu.VMEM((count, ncol, BLOCK, BLOCK), jnp.bfloat16),
            pltpu.SemaphoreType.DMA((count, ncol)),
        ],
        out_shape=jax.ShapeDtypeStruct(out.shape, out.dtype),
        input_output_aliases={3 + shard_count: 0},
        compiler_params=pltpu.CompilerParams(vmem_limit_bytes=4 * (ncol + count) * rows * width + (4 << 20)),
        cost_estimate=pl.CostEstimate(
            flops=4 * count * ncol * BLOCK * BLOCK * width,
            bytes_accessed=4 * count * (ncol * BLOCK + rows) * width,
            transcendentals=0,
        ),
        name="blocks",
    )(tab, occ, vir, *row_shards, *amp_b, *int_b, out)


def gather_cols(amplitudes, integrals, ncol):
    arrays, spots = [amplitudes, integrals], {0: ((0, 0), (1, 0))}
    bit = ncol // 2
    while bit:
        pairs = [(c, c ^ bit) for c in range(ncol)]
        if len(arrays) == 2:
            spots[bit] = ((2, 0), (3, 0))
            arrays.append(lax.ppermute(amplitudes, "col", pairs))
            arrays.append(lax.ppermute(after(integrals, arrays[2]), "col", pairs))
        else:
            for n, array in enumerate(list(arrays)):
                arrays.append(lax.ppermute(array, "col", pairs))
            known = len(arrays) // 2
            spots.update({m ^ bit: tuple((n + known, q) for n, q in at) for m, at in spots.items()})
        bit //= 2
    return arrays, spots


def after(x, gate):
    return x if gate is None else lax.optimization_barrier((x, gate))[0]


def shards(amplitudes, integrals, block_mask, occ_energy, vir_energy):
    nrow = lax.axis_size("row")
    ncol = lax.axis_size("col")
    split = SHARD_BLOCKS
    limit = min(TILES, nrow * ncol)
    where = jnp.stack([lax.axis_index("row"), lax.axis_index("col")]).astype(jnp.int32)
    order = ring_order(nrow)
    spot = {row: at for at, row in enumerate(order)}
    source = np.array([order[(spot[row] - s) % nrow] for row in range(nrow) for s in range(nrow)], np.int32)
    ahead = [(order[p], order[(p + 1) % nrow]) for p in range(nrow)]
    behind = [(b, a) for a, b in ahead]
    tab, out = slot_table(where, source, block_mask, ncol, nrow, split, limit)
    vir = vir_energy.reshape(-1, BLOCK)

    def update(hops, amp_b, int_b, out):
        return step(hops, spots, tab, occ_energy, vir, row_shards, amp_b, int_b, out, ncol, nrow, split)

    far = nrow // 2
    amp_up = amp_down = amplitudes
    int_up = int_down = integrals
    waiting = []
    for s in range(1, far + 1):
        last = (amp_up, amp_down, int_up, int_down)
        gate = tab if s == 3 else None
        amp_up = lax.ppermute(after(amp_up, gate), "row", ahead)
        int_down = lax.ppermute(after(int_down, gate), "row", behind)
        if s < nrow - s:
            int_up = lax.ppermute(int_up, "row", ahead)
            amp_down = lax.ppermute(amp_down, "row", behind)
        if s == min(3, far):
            row_shards, spots = gather_cols(amplitudes, integrals, ncol)
        waiting.append((s - 1, last[0], last[2]))
        if s >= 2:
            waiting.append((nrow - s + 1, last[1], last[3]))
        if s >= min(3, far):
            hops, amp_b, int_b = zip(*waiting)
            out = update(hops, amp_b, int_b, out)
            waiting = []
    if far == nrow - far:
        out = update((far,), (amp_up,), (int_down,), out)
    else:
        out = update((far, nrow - far), (amp_up, amp_down), (int_up, int_down), out)
    return out[None, None]


def solution(mesh):
    in_specs = (P(("row", "col"), None), P(("row", "col"), None), P("row", None), P(), P())
    out_specs = P("row", "col", None, None, None)
    return jax.shard_map(shards, mesh=mesh, in_specs=in_specs, out_specs=out_specs, check_vma=False)
```
